256 devices in a mesh: ctx: 32 (over x, y, core), tp: 8 (over z).
Axes of the slice: x: 4, y: 4, z: 8, core: 2. Of those that a mesh axis runs over, the one named last changes fastest.
Arguments:
- ctx_queries: bfloat16 [16384, 8192], P('ctx', 'tp'), may hold values from -100 to 100
- ctx_keyvals: bfloat16 [2, 16384, 1024], P(None, 'ctx', 'tp'), may hold values from -4 to 4
- block_map: int32 [64], replicated, may hold values from 0 to 63, as said below
- window_reach: int32 [2], replicated, may hold values from 16 to 32
- win_queries: bfloat16 [2, 256, 8192], P(None, None, 'tp'), may hold values from -100 to 100
- win_keyvals: bfloat16 [2, 2, 256, 1024], P(None, None, None, 'tp'), may hold values from -4 to 4
- out_weight: bfloat16 [8192, 8192], P('tp', 'ctx'), may hold values from -0.25 to 0.25
Outputs:
- context_attn: bfloat16 [16384, 8192], P('ctx', 'tp')
- window_proj: float32 [512, 8192], P('tp', 'ctx')
The draws below stay inside these ranges and needn't reach their ends.
Inputs may be any that keep to these rules, and one draw needn't show every extreme that they name: `block_map`: each logical block of 0 to 63 appears exactly once; blocks c * 32 to (c + 1) * 32 - 1 make context c; of the row blocks 2 i and 2 i + 1 one holds a block of context 0 and the other a block of context 1.
All inputs are finite; a program needn't handle non-finite values.
Results may differ from the reference program's by a relative error of at most 0.0035.
Values may be sent and summed in bfloat16 or wider, within the bound.
No kernel may reach another device: no remote copies, remote signals or barrier semaphores. Data moves between devices by JAX's collectives and lax.ppermute only.
A program may use at most 192 MiB of HBM per device.

```python
import math
import jax
import jax.numpy as jnp
from jax import lax

D = 8192
HQ = 64
HK = 8
HD = 128
BLK = 256
QW = 256
NB = 32


def marked_keys(key, salt_value, array_shape):
    base = jax.random.fold_in(key, salt_value)
    keys_drawn = jnp.clip(jax.random.normal(jax.random.fold_in(base, 1), array_shape, jnp.float32), -4.0, 4.0)
    return keys_drawn


def draw_block_map(key, part):
    key = jax.random.fold_in(key, 11)
    first_places = jax.random.permutation(jax.random.fold_in(key, 1), NB).astype(jnp.int32)
    second_places = jax.random.permutation(jax.random.fold_in(key, 2), NB).astype(jnp.int32) + NB
    flips = jax.random.randint(jax.random.fold_in(key, 3), (NB,), 0, 2).astype(jnp.int32)
    lead_slot = jnp.where(flips == 0, first_places, second_places)
    trail_slot = jnp.where(flips == 0, second_places, first_places)
    return jnp.stack([lead_slot, trail_slot], axis=1).reshape(2 * NB).astype(jnp.int32)


def draw_ctx_queries(key, part):
    row_total = 2 * NB * BLK
    key = jax.random.fold_in(key, 3)
    return jnp.clip(2.0 * jax.random.normal(key, (row_total, HQ * HD), jnp.float32), -8.0, 8.0).astype(jnp.bfloat16)


def draw_ctx_keyvals(key, part):
    row_total = 2 * NB * BLK
    shared_keys = marked_keys(key, 101, (row_total, HK * HD))
    key = jax.random.fold_in(key, 5)
    values = jnp.clip(jax.random.normal(key, (row_total, HK * HD), jnp.float32), -4.0, 4.0)
    return jnp.stack([shared_keys, values], axis=0).astype(jnp.bfloat16)


def draw_win_queries(key, part):
    key = jax.random.fold_in(key, 7)
    return jnp.clip(2.0 * jax.random.normal(key, (2, QW, HQ * HD), jnp.float32), -8.0, 8.0).astype(jnp.bfloat16)


def draw_win_keyvals(key, part):
    shared_keys = marked_keys(key, 202, (2, QW, HK * HD))
    key = jax.random.fold_in(key, 9)
    values = jnp.clip(jax.random.normal(key, (2, QW, HK * HD), jnp.float32), -4.0, 4.0)
    return jnp.stack([shared_keys, values], axis=1).astype(jnp.bfloat16)


def block_scale(stream_key, extent, cuts, low, largest):
    loudness, own = 1.0, jax.random.fold_in(stream_key, 6)
    for dim, blocks in cuts:
        heights = jnp.exp(jax.random.uniform(jax.random.fold_in(own, dim), (blocks,), jnp.float32, low / len(cuts), largest / len(cuts)))
        loudness = loudness * jnp.repeat(heights, extent[dim] // blocks).reshape([-1 if axis == dim else 1 for axis in range(len(extent))])
    return loudness


def normal_values(key, shape, scale, limit, cuts=(), kind=jnp.bfloat16):
    factor_of = block_scale(key, shape, cuts, -0.22, 0.18) if cuts else 1.0
    result = jax.random.normal(key, shape, jnp.float32) * scale * factor_of
    return jnp.minimum(jnp.maximum(result, -limit), limit).astype(kind)


def setup_inputs(seed: int = 0) -> dict:
    seeds = jax.random.split(jax.random.key(seed), 8)
    return {
        "ctx_queries": draw_ctx_queries(jax.random.fold_in(seeds[7], 71), 0),
        "ctx_keyvals": draw_ctx_keyvals(jax.random.fold_in(seeds[7], 71), 0),
        "block_map": draw_block_map(jax.random.fold_in(seeds[7], 71), 0),
        "window_reach": jax.random.randint(seeds[3], (2,), NB // 2, NB + 1).astype(jnp.int32),
        "win_queries": draw_win_queries(jax.random.fold_in(seeds[7], 71), 0),
        "win_keyvals": draw_win_keyvals(jax.random.fold_in(seeds[7], 71), 0),
        "out_weight": normal_values(seeds[6], (HQ * HD, D), (HQ * HD // 16) ** -0.5, 0.25, ((0, 8), (1, 32))),
    }


masked_score = -1e+30

def partial_softmax(query_rows, key_rows, value_rows, count_mask):
    row_count = query_rows.shape[0]
    key_heads = key_rows.shape[1] // HD
    groups = HQ // HK
    query_split = query_rows.astype(jnp.float32).reshape(row_count, key_heads, groups, HD)
    key_split = key_rows.astype(jnp.float32).reshape(-1, key_heads, HD)
    value_split = value_rows.astype(jnp.float32).reshape(-1, key_heads, HD)
    scores = jnp.einsum('rhgd,khd->rhgk', query_split, key_split) / math.sqrt(HD)
    live_mask = count_mask[:, None, None, :]
    scores = jnp.where(live_mask, scores, masked_score)
    row_top = lax.optimization_barrier(jnp.max(scores, axis=-1))
    weights = jnp.where(live_mask, jnp.exp(scores - row_top[..., None]), 0.0)
    row_total = lax.optimization_barrier(jnp.sum(weights, axis=-1))
    weights_low = lax.optimization_barrier(weights.astype(jnp.bfloat16)).astype(jnp.float32)
    weighted = jnp.einsum('rhgk,khd->rhgd', weights_low, value_split)
    return (row_top.reshape(row_count, -1), row_total.reshape(row_count, -1), weighted.reshape(row_count, -1))

def combine_parts(former, latter):
    joined_top = jnp.maximum(former[0], latter[0])
    former_lift = jnp.exp(former[0] - joined_top)
    latter_lift = jnp.exp(latter[0] - joined_top)
    joined_total = former[1] * former_lift + latter[1] * latter_lift
    joined_sum = former[2] * jnp.repeat(former_lift, HD, axis=-1) + latter[2] * jnp.repeat(latter_lift, HD, axis=-1)
    return (joined_top, joined_total, joined_sum)

def finish_rows(parts):
    return parts[2] / jnp.repeat(parts[1], HD, axis=-1)

def anchor_slots(block_map):
    slot_ids = jnp.arange(block_map.shape[0], dtype=jnp.int32)
    firsts = jnp.arange(2, dtype=jnp.int32) * NB
    hits = (block_map[None, :] == firsts[:, None]).astype(jnp.int32)
    return lax.optimization_barrier(jnp.sum(hits * slot_ids[None, :], axis=1)).astype(jnp.int32)

def lower_mask(length):
    return jnp.arange(length)[:, None] >= jnp.arange(length)[None, :]

def reference(ctx_queries, ctx_keyvals, block_map, window_reach, win_queries, win_keyvals, out_weight):
    anchors = anchor_slots(block_map)
    causal = lower_mask(BLK)
    all_keys = ctx_keyvals[0]
    all_values = ctx_keyvals[1]

    def block_out(slot_index):
        block_id = block_map[slot_index]
        context_id = block_id // NB
        anchor_id = anchors[context_id]
        query_rows = lax.dynamic_slice_in_dim(ctx_queries, slot_index * BLK, BLK, 0)
        key_rows = jnp.concatenate([lax.dynamic_slice_in_dim(all_keys, anchor_id * BLK, BLK, 0), lax.dynamic_slice_in_dim(all_keys, slot_index * BLK, BLK, 0)], 0)
        value_rows = jnp.concatenate([lax.dynamic_slice_in_dim(all_values, anchor_id * BLK, BLK, 0), lax.dynamic_slice_in_dim(all_values, slot_index * BLK, BLK, 0)], 0)
        anchor_seen = jnp.broadcast_to(block_id % NB != 0, (BLK, BLK))
        count_mask = jnp.concatenate([anchor_seen, causal], axis=1)
        return finish_rows(partial_softmax(query_rows, key_rows, value_rows, count_mask)).astype(jnp.bfloat16)
    context_attn = lax.map(block_out, jnp.arange(2 * NB, dtype=jnp.int32)).reshape(2 * NB * BLK, HQ * HD)
    window_causal = lower_mask(QW)
    window_rows = []
    for context_id in range(2):
        query_rows = win_queries[context_id]
        opening = partial_softmax(query_rows, win_keyvals[context_id, 0], win_keyvals[context_id, 1], window_causal)

        def advance(carry, slot_index):
            block_id = block_map[slot_index]
            live_block = (block_id // NB == context_id) & (block_id % NB < window_reach[context_id])
            key_rows = lax.dynamic_slice_in_dim(all_keys, slot_index * BLK, BLK, 0)
            value_rows = lax.dynamic_slice_in_dim(all_values, slot_index * BLK, BLK, 0)
            block_part = partial_softmax(query_rows, key_rows, value_rows, jnp.broadcast_to(live_block, (QW, BLK)))
            return (combine_parts(carry, block_part), None)
        merged, unused = lax.scan(advance, opening, jnp.arange(2 * NB, dtype=jnp.int32))
        window_rows.append(finish_rows(merged).astype(jnp.bfloat16))
    window_attn = jnp.concatenate(window_rows, 0)
    window_proj = jnp.dot(window_attn, out_weight, preferred_element_type=jnp.float32)
    return (context_attn, window_proj)
```

```python
import math

import jax
import jax.numpy as jnp
from jax import lax
from jax.experimental import pallas as pl
from jax.experimental.pallas import tpu as pltpu
from jax.sharding import PartitionSpec as P

HD = 128
HEADS = 8
BLK = 256
NB = 32
CHIPS = 16
HALF = 128
STAT = 16
PIECE = 32
SCALE = 1.0 / math.sqrt(HD)
masked_score = -1e30

SEND_ROWS = HALF + STAT + PIECE
SHARE_ROWS = HALF + PIECE

same_core = [[chip * 2 + core for chip in range(CHIPS)] for core in range(2)]
core_swap = [(device, device ^ 1) for device in range(2 * CHIPS)]

smem = pl.BlockSpec(memory_space=pltpu.SMEM)
vmem = pl.BlockSpec(memory_space=pltpu.VMEM)


def params():
    return pltpu.CompilerParams(vmem_limit_bytes=40 * 2**20)


def cost(flops, exps, size):
    return pl.CostEstimate(flops=flops, transcendentals=exps, bytes_accessed=size)


def split_three(value):
    high = value.astype(jnp.bfloat16)
    rest = value - high.astype(jnp.float32)
    middle = rest.astype(jnp.bfloat16)
    low = (rest - middle.astype(jnp.float32)).astype(jnp.bfloat16)
    return high, middle, low


def dot_nt(left, right):
    return lax.dot_general(
        left, right, (((1,), (1,)), ((), ())), preferred_element_type=jnp.float32
    )


def column_softmax(raw):
    top = jnp.max(raw, axis=0, keepdims=True)
    weights = jnp.exp((raw - top) * SCALE)
    return top * SCALE, jnp.sum(weights, axis=0, keepdims=True), weights


def window_kernel(map_ref, reach_ref, query_ref, own_ref, other_ref, send_ref):
    position = lax.axis_index("ctx")
    core = position % 2
    partner = position + 1 - 2 * core
    reach = reach_ref[core]
    blocks = []
    for ref, device in ((own_ref, position), (other_ref, partner)):
        slot = jnp.where(map_ref[2 * device] // NB == core, 0, 1)
        place = map_ref[2 * device + slot] - NB * core
        rows = pl.ds(pl.multiple_of(slot * BLK, BLK), BLK)
        keys = ref[0, rows, :]
        values = ref[1, rows, :]
        blocks.append((place < reach, place, keys, values, values.T))
    for head in range(HEADS):
        query = query_ref[core, :, head * HD : (head + 1) * HD]
        parts = []
        for live, _, keys, _, values_t in blocks:
            top, total, weights = column_softmax(dot_nt(keys, query))
            weighted = jnp.dot(
                values_t, weights.astype(jnp.bfloat16), preferred_element_type=jnp.float32
            )
            parts.append((jnp.where(live, top, masked_score), total, weighted, live))
        joined = jnp.maximum(parts[0][0], parts[1][0])
        lifts = [jnp.where(part[3], jnp.exp(part[0] - joined), 0.0) for part in parts]
        total = parts[0][1] * lifts[0] + parts[1][1] * lifts[1]
        some = total > 0.0
        inverse = jnp.where(some, 1.0 / jnp.where(some, total, 1.0), 0.0)
        level = jnp.where(some, joined + jnp.log(jnp.where(some, total, 1.0)), masked_score)
        mean = parts[0][2] * (lifts[0] * inverse) + parts[1][2] * (lifts[1] * inverse)
        mean = mean.astype(jnp.bfloat16)
        high, middle, low = split_three(level)
        row = lax.broadcasted_iota(jnp.int32, (STAT, BLK), 0)
        stats = jnp.where(
            row == 0,
            high.astype(jnp.float32),
            jnp.where(
                row == 1,
                middle.astype(jnp.float32),
                jnp.where(row == 2, low.astype(jnp.float32), 0.0),
            ),
        ).astype(jnp.bfloat16)
        for half in range(2):
            lanes = slice(half * HALF, (half + 1) * HALF)
            send_ref[2 * head + half, :HALF, :] = mean[:, lanes]
            send_ref[2 * head + half, HALF : HALF + STAT, :] = stats[:, lanes]
    first = blocks[0][1] == 0
    for member in range(2):
        block = jnp.where(first, blocks[0][2 + member], blocks[1][2 + member])
        send_ref[8 * member : 8 * member + 8, HALF + STAT :, :] = block.reshape(8, PIECE, HD)


def own_kernel(query_ref, keyval_ref, mean_ref, level_ref):
    position = lax.axis_index("ctx")
    core = position % 2
    chip = position // 2
    half = chip % 2
    rows = pl.ds(pl.multiple_of(half * HALF, HALF), HALF)
    lanes = pl.ds(pl.multiple_of(chip // 2 * HD, HD), HD)
    query = query_ref[core, rows, lanes]
    raw = dot_nt(keyval_ref[core, 0], query)
    key = lax.broadcasted_iota(jnp.int32, raw.shape, 0)
    row = lax.broadcasted_iota(jnp.int32, raw.shape, 1) + half * HALF
    live = key <= row
    raw = jnp.where(live, raw, masked_score)
    top = jnp.max(raw, axis=0, keepdims=True)
    weights = jnp.where(live, jnp.exp((raw - top) * SCALE), 0.0)
    total = jnp.sum(weights, axis=0, keepdims=True)
    weighted = jnp.dot(
        keyval_ref[core, 1].T, weights.astype(jnp.bfloat16), preferred_element_type=jnp.float32
    )
    mean_ref[...] = weighted / total
    level_ref[...] = jnp.broadcast_to(top * SCALE + jnp.log(total), level_ref.shape)


def combine_kernel(map_ref, got_ref, mean_ref, level_ref, share_ref):
    core = lax.axis_index("ctx") % 2

    def look(slot, found):
        return jnp.where(map_ref[slot] == core * NB, slot, found)

    holder = lax.fori_loop(0, 2 * NB, look, jnp.int32(0)) // 4
    levels = [level_ref[0:1, :]]
    for source in range(CHIPS):
        stats = got_ref[source, HALF : HALF + STAT, :].astype(jnp.float32)
        levels.append(stats[0:1] + stats[1:2] + stats[2:3])
    top = levels[0]
    for level in levels[1:]:
        top = jnp.maximum(top, level)
    lift = jnp.exp(levels[0] - top)
    total = lift
    joined = mean_ref[...] * lift
    for source in range(CHIPS):
        lift = jnp.exp(levels[source + 1] - top)
        total = total + lift
        joined = joined + got_ref[source, :HALF, :].astype(jnp.float32) * lift
    result = (joined / total).T.astype(jnp.bfloat16)
    piece = got_ref[holder, HALF + STAT :, :]
    for target in range(CHIPS):
        share_ref[target, :HALF, :] = result
        share_ref[target, HALF:, :] = piece


def project_kernel(own_ref, other_ref, weight_ref, out_ref):
    core = lax.axis_index("ctx") % 2
    for ref, context in ((own_ref, core), (other_ref, 1 - core)):
        for half in range(2):
            rows = jnp.concatenate(
                [ref[2 * head + half, :HALF, :] for head in range(HEADS)], axis=1
            )
            result = jnp.dot(rows, weight_ref[...], preferred_element_type=jnp.float32)
            out_ref[pl.ds(context * 4 + half * 2, 2)] = result.reshape(2, 64, BLK)


STEP_HEADS = 4


def block_kernel(map_ref, query_ref, keyval_ref, own_ref, other_ref, out_ref):
    position = lax.axis_index("ctx")
    core = position % 2
    slot = pl.program_id(0)
    block = map_ref[2 * position + slot]
    mine = block // NB == core
    seen = block % NB != 0

    def anchor(member):
        taken = slice(8 * member, 8 * member + 8)
        own = own_ref[taken, HALF:, :].reshape(BLK, HD)
        other = other_ref[taken, HALF:, :].reshape(BLK, HD)
        return jnp.where(mine, own, other)

    keys = jnp.concatenate([anchor(0), keyval_ref[0]], axis=0)
    values = jnp.concatenate([anchor(1), keyval_ref[1]], axis=0)
    key = lax.broadcasted_iota(jnp.int32, (BLK, 2 * BLK), 1)
    row = lax.broadcasted_iota(jnp.int32, (BLK, 2 * BLK), 0) + BLK
    first_key = jnp.where(seen, 0, BLK)
    live = (key <= row) & (key >= first_key)
    for head in range(STEP_HEADS):
        lanes = slice(head * HD, (head + 1) * HD)
        raw = jnp.where(live, dot_nt(query_ref[:, lanes], keys), masked_score)
        top = jnp.max(raw, axis=1, keepdims=True)
        weights = jnp.where(live, jnp.exp((raw - top) * SCALE), 0.0)
        total = jnp.sum(weights, axis=1, keepdims=True)
        weighted = jnp.dot(
            weights.astype(jnp.bfloat16), values, preferred_element_type=jnp.float32
        )
        out_ref[:, lanes] = (weighted / total).astype(jnp.bfloat16)


def shaped(shape, dtype):
    return jax.ShapeDtypeStruct(shape, dtype)


def on_device(
    ctx_queries, ctx_keyvals, block_map, window_reach, win_queries, win_keyvals, out_weight
):
    other_keyvals = lax.ppermute(ctx_keyvals, "ctx", core_swap)
    send = pl.pallas_call(
        window_kernel,
        out_shape=shaped((CHIPS, SEND_ROWS, HD), jnp.bfloat16),
        in_specs=[smem, smem, vmem, vmem, vmem],
        out_specs=vmem,
        compiler_params=params(),
        cost_estimate=cost(2**29, 2**20, 2**21),
        name="window_parts",
    )(block_map, window_reach, win_queries, ctx_keyvals, other_keyvals)
    got = lax.all_to_all(send, "ctx", 0, 0, axis_index_groups=same_core, tiled=True)
    own_mean, own_level = pl.pallas_call(
        own_kernel,
        out_shape=(shaped((HD, HALF), jnp.float32), shaped((8, HALF), jnp.float32)),
        in_specs=[vmem, vmem],
        out_specs=(vmem, vmem),
        compiler_params=params(),
        cost_estimate=cost(2**24, 2**15, 2**20),
        name="window_own",
    )(win_queries, win_keyvals)
    share = pl.pallas_call(
        combine_kernel,
        out_shape=shaped((CHIPS, SHARE_ROWS, HD), jnp.bfloat16),
        in_specs=[smem, vmem, vmem, vmem],
        out_specs=vmem,
        compiler_params=params(),
        cost_estimate=cost(2**20, 2**12, 2**20),
        name="window_join",
    )(block_map, got, own_mean, own_level)
    rows_own = lax.all_to_all(share, "ctx", 0, 0, axis_index_groups=same_core, tiled=True)
    rows_other = lax.ppermute(rows_own, "ctx", core_swap)
    shares = pl.pallas_call(
        project_kernel,
        out_shape=shaped((8, 64, BLK), jnp.float32),
        in_specs=[vmem, vmem, vmem],
        out_specs=vmem,
        compiler_params=params(),
        cost_estimate=cost(2**28, 0, 2**21),
        name="project",
    )(rows_own, rows_other, out_weight)
    summands = lax.all_to_all(shares, "tp", 0, 0, tiled=True)
    context_attn = pl.pallas_call(
        block_kernel,
        out_shape=shaped((2 * BLK, HEADS * HD), jnp.bfloat16),
        grid=(2, HEADS // STEP_HEADS),
        in_specs=[
            smem,
            pl.BlockSpec((BLK, STEP_HEADS * HD), lambda slot, step: (slot, step)),
            pl.BlockSpec((2, BLK, HD), lambda slot, step: (0, slot, 0)),
            pl.BlockSpec((CHIPS, SHARE_ROWS, HD), lambda slot, step: (0, 0, 0)),
            pl.BlockSpec((CHIPS, SHARE_ROWS, HD), lambda slot, step: (0, 0, 0)),
        ],
        out_specs=pl.BlockSpec((BLK, STEP_HEADS * HD), lambda slot, step: (slot, step)),
        compiler_params=params(),
        cost_estimate=cost(2**30, 2**21, 2**22),
        name="block_attention",
    )(block_map, ctx_queries, ctx_keyvals, rows_own, rows_other)
    window_proj = jnp.sum(summands, axis=0)
    return (context_attn, window_proj)


def solution(mesh):
    return jax.shard_map(
        on_device,
        mesh=mesh,
        in_specs=(
            P("ctx", "tp"),
            P(None, "ctx", "tp"),
            P(),
            P(),
            P(None, None, "tp"),
            P(None, None, None, "tp"),
            P("tp", "ctx"),
        ),
        out_specs=(P("ctx", "tp"), P("tp", "ctx")),
        check_vma=False,
    )
```

```python
import math

import jax
import jax.numpy as jnp
from jax import lax
from jax.experimental import pallas as pl
from jax.experimental.pallas import tpu as pltpu
from jax.sharding import PartitionSpec as P

HD = 128
HEADS = 8
BLK = 256
NB = 32
CHIPS = 16
HALF = 128
STAT = 16
PIECE = 32
SCALE = 1.0 / math.sqrt(HD)
SCALE2 = SCALE * math.log2(math.e)
masked_score = -1e30

SEND_ROWS = HALF + STAT + PIECE
SHARE_ROWS = HALF + PIECE

same_core = [[chip * 2 + core for chip in range(CHIPS)] for core in range(2)]
core_swap = [(device, device ^ 1) for device in range(2 * CHIPS)]

smem = pl.BlockSpec(memory_space=pltpu.SMEM)
vmem = pl.BlockSpec(memory_space=pltpu.VMEM)
hbm = pl.BlockSpec(memory_space=pltpu.HBM)


def params(room=40):
    return pltpu.CompilerParams(vmem_limit_bytes=room * 2**20)


def cost(flops, exps, size):
    return pl.CostEstimate(flops=flops, transcendentals=exps, bytes_accessed=size)


def split_three(value):
    high = value.astype(jnp.bfloat16)
    rest = value - high.astype(jnp.float32)
    middle = rest.astype(jnp.bfloat16)
    low = (rest - middle.astype(jnp.float32)).astype(jnp.bfloat16)
    return high, middle, low


def dot_nt(left, right):
    return lax.dot_general(
        left, right, (((1,), (1,)), ((), ())), preferred_element_type=jnp.float32
    )


def row_softmax(raw):
    top = jnp.max(raw, axis=1, keepdims=True)
    weights = jnp.exp2((raw - top) * SCALE2)
    return top * SCALE, jnp.sum(weights, axis=1, keepdims=True), weights


def weigh(weights, values):
    return jnp.dot(weights.astype(jnp.bfloat16), values, preferred_element_type=jnp.float32)


def find_block(map_ref, device, core):
    slot = jnp.where(map_ref[2 * device] // NB == core, 0, 1)
    place = map_ref[2 * device + slot] - NB * core
    return place, pl.ds(pl.multiple_of(slot * BLK, BLK), BLK)


def block_parts(query_ref, keys, values, sum_ref):
    lane = lax.broadcasted_iota(jnp.int32, (BLK, HD), 1)
    tops = jnp.zeros((BLK, HD), jnp.float32)
    totals = jnp.zeros((BLK, HD), jnp.float32)
    for head in range(HEADS):
        lanes = slice(head * HD, (head + 1) * HD)
        top, total, weights = row_softmax(dot_nt(query_ref[:, lanes], keys))
        sum_ref[:, lanes] = weigh(weights, values)
        tops = jnp.where(lane == head, top, tops)
        totals = jnp.where(lane == head, total, totals)
    return tops, totals


def first_kernel(
    map_hbm,
    reach_hbm,
    query_hbm,
    keyval_hbm,
    window_hbm,
    query_ref,
    sum_ref,
    top_ref,
    total_ref,
    mean_ref,
    level_ref,
    info_ref,
    keyval_ref,
    window_ref,
    map_ref,
    reach_ref,
    done,
):
    position = lax.axis_index("ctx")
    core = position % 2
    chip = position // 2
    copies = [
        pltpu.make_async_copy(source, target, done.at[number])
        for number, (source, target) in enumerate(
            (
                (map_hbm, map_ref),
                (reach_hbm, reach_ref),
                (keyval_hbm, keyval_ref),
                (query_hbm.at[core], query_ref),
                (window_hbm.at[core], window_ref),
            )
        )
    ]
    for copy in copies:
        copy.start()
    for copy in copies:
        copy.wait()
    partner = position + 1 - 2 * core
    reach = reach_ref[core]
    place, rows = find_block(map_ref, position, core)
    other_place, _ = find_block(map_ref, partner, core)
    holder = jnp.int32(0)
    for slot in range(2 * NB):
        holder = jnp.where(map_ref[slot] == core * NB, slot // 4, holder)
    info_ref[0] = holder
    info_ref[1] = jnp.where(place < reach, 1, 0)
    info_ref[2] = jnp.where(other_place < reach, 1, 0)
    info_ref[3] = place
    info_ref[4] = jnp.where(map_ref[2 * partner] // NB == core, 0, 1)
    info_ref[5] = jnp.where(map_ref[2 * position] // NB == core, 0, 1)
    info_ref[6] = map_ref[2 * position]
    info_ref[7] = map_ref[2 * position + 1]
    top_ref[...], total_ref[...] = block_parts(
        query_ref, keyval_ref[0, rows, :], keyval_ref[1, rows, :], sum_ref
    )
    half = chip % 2
    query_rows = pl.ds(pl.multiple_of(half * HALF, HALF), HALF)
    query_lanes = pl.ds(pl.multiple_of(chip // 2 * HD, HD), HD)
    raw = dot_nt(query_ref[query_rows, query_lanes], window_ref[0])
    key = lax.broadcasted_iota(jnp.int32, raw.shape, 1)
    row = lax.broadcasted_iota(jnp.int32, raw.shape, 0) + half * HALF
    live = key <= row
    raw = jnp.where(live, raw, masked_score)
    top, _, weights = row_softmax(raw)
    weights = jnp.where(live, weights, 0.0)
    total = jnp.sum(weights, axis=1, keepdims=True)
    mean_ref[...] = weigh(weights, window_ref[1]) / total
    level = jnp.broadcast_to(top + jnp.log(total), (HALF, HALF)).T
    level_ref[...] = level[:8]


def second_kernel(
    info_ref,
    query_ref,
    sum_ref,
    top_ref,
    total_ref,
    own_ref,
    other_ref,
    send_ref,
    second_ref,
):
    own_rows = pl.ds(pl.multiple_of(info_ref[5] * BLK, BLK), BLK)
    other_rows = pl.ds(pl.multiple_of(info_ref[4] * BLK, BLK), BLK)
    first = info_ref[3] == 0
    for member in range(2):
        block = jnp.where(first, own_ref[member, own_rows, :], other_ref[member, other_rows, :])
        send_ref[8 * member : 8 * member + 8, HALF + STAT :, :] = block.reshape(8, PIECE, HD)
    tops, totals = block_parts(
        query_ref, other_ref[0, other_rows, :], other_ref[1, other_rows, :], second_ref
    )
    lives = (info_ref[1] == 1, info_ref[2] == 1)
    tops = [
        jnp.where(live, top, masked_score) for live, top in zip(lives, (top_ref[...], tops))
    ]
    joined = jnp.maximum(tops[0], tops[1])
    lifts = [jnp.where(live, jnp.exp(top - joined), 0.0) for live, top in zip(lives, tops)]
    total = total_ref[...] * lifts[0] + totals * lifts[1]
    some = total > 0.0
    safe = jnp.where(some, total, 1.0)
    inverse = jnp.where(some, 1.0 / safe, 0.0)
    lifts = [lift * inverse for lift in lifts]
    level = jnp.where(some, joined + jnp.log(safe), masked_score).T[:HEADS]
    pieces = [piece.astype(jnp.float32) for piece in split_three(level)]
    row = lax.broadcasted_iota(jnp.int32, (STAT, BLK), 0)
    for head in range(HEADS):
        lanes = slice(head * HD, (head + 1) * HD)
        mean = (
            sum_ref[:, lanes] * lifts[0][:, head : head + 1]
            + second_ref[:, lanes] * lifts[1][:, head : head + 1]
        ).astype(jnp.bfloat16)
        stats = jnp.zeros((STAT, BLK), jnp.float32)
        for number, piece in enumerate(pieces):
            stats = jnp.where(row == number, piece[head : head + 1], stats)
        stats = stats.astype(jnp.bfloat16)
        for half in range(2):
            rows = slice(half * HALF, (half + 1) * HALF)
            send_ref[2 * head + half, :HALF, :] = mean[rows]
            send_ref[2 * head + half, HALF : HALF + STAT, :] = stats[:, rows]


def combine_kernel(info_ref, got_ref, mean_ref, level_ref, share_ref):
    levels = []
    for source in range(CHIPS):
        stats = got_ref[source, HALF : HALF + STAT, :].astype(jnp.float32)
        levels.append(stats[0:1] + stats[1:2] + stats[2:3])
    levels.append(level_ref[0:1, :])
    levels = jnp.concatenate(levels, axis=0)
    lifts = jnp.exp(levels - jnp.max(levels, axis=0, keepdims=True))
    lifts = lifts / jnp.sum(lifts, axis=0, keepdims=True)
    blank = jnp.zeros((HALF - CHIPS - 1, HALF), jnp.float32)
    lifts = jnp.concatenate([lifts, blank], axis=0).T
    joined = mean_ref[...] * lifts[:, CHIPS : CHIPS + 1]
    for source in range(CHIPS):
        part = got_ref[source, :HALF, :].astype(jnp.float32)
        joined = joined + part * lifts[:, source : source + 1]
    result = joined.astype(jnp.bfloat16)
    piece = got_ref[info_ref[0], HALF + STAT :, :]
    for target in range(CHIPS):
        share_ref[target, :HALF, :] = result
        share_ref[target, HALF:, :] = piece


def project_kernel(own_ref, other_ref, weight_ref, out_ref):
    core = lax.axis_index("ctx") % 2
    rows = jnp.concatenate(
        [
            jnp.concatenate([ref[2 * head + half, :HALF, :] for head in range(HEADS)], axis=1)
            for ref in (own_ref, other_ref)
            for half in range(2)
        ],
        axis=0,
    )
    result = jnp.dot(rows, weight_ref[...], preferred_element_type=jnp.float32)
    result = result.reshape(8, 64, BLK).astype(out_ref.dtype)
    out_ref[pl.ds(core * 4, 4)] = result[:4]
    out_ref[pl.ds(4 - core * 4, 4)] = result[4:]


STEP_HEADS = 4


def block_kernel(info_ref, query_ref, keyval_ref, own_ref, other_ref, out_ref):
    core = lax.axis_index("ctx") % 2
    block = info_ref[6 + pl.program_id(0)]
    mine = block // NB == core
    seen = block % NB != 0

    def anchor(member):
        taken = slice(8 * member, 8 * member + 8)
        own = own_ref[taken, HALF:, :].reshape(BLK, HD)
        other = other_ref[taken, HALF:, :].reshape(BLK, HD)
        return jnp.where(mine, own, other)

    keys = jnp.concatenate([anchor(0), keyval_ref[0]], axis=0)
    values = jnp.concatenate([anchor(1), keyval_ref[1]], axis=0)
    key = lax.broadcasted_iota(jnp.int32, (BLK, 2 * BLK), 1)
    row = lax.broadcasted_iota(jnp.int32, (BLK, 2 * BLK), 0) + BLK
    first_key = jnp.where(seen, 0, BLK)
    live = (key <= row) & (key >= first_key)
    for head in range(STEP_HEADS):
        lanes = slice(head * HD, (head + 1) * HD)
        raw = jnp.where(live, dot_nt(query_ref[:, lanes], keys), masked_score)
        _, total, weights = row_softmax(raw)
        out_ref[:, lanes] = (weigh(weights, values) / total).astype(jnp.bfloat16)


def far(array):
    return pltpu.with_memory_space_constraint(array, pltpu.HBM)


def shaped(shape, dtype):
    return jax.ShapeDtypeStruct(shape, dtype)


def on_device(
    ctx_queries, ctx_keyvals, block_map, window_reach, win_queries, win_keyvals, out_weight
):
    other_keyvals = lax.ppermute(ctx_keyvals, "ctx", core_swap)
    queries, sums, tops, totals, own_mean, own_level, info = pl.pallas_call(
        first_kernel,
        out_shape=(
            shaped((BLK, HEADS * HD), jnp.bfloat16),
            shaped((BLK, HEADS * HD), jnp.float32),
            shaped((BLK, HD), jnp.float32),
            shaped((BLK, HD), jnp.float32),
            shaped((HALF, HD), jnp.float32),
            shaped((8, HALF), jnp.float32),
            shaped((8,), jnp.int32),
        ),
        in_specs=[hbm] * 5,
        out_specs=(vmem,) * 6 + (smem,),
        scratch_shapes=[
            pltpu.VMEM((2, 2 * BLK, HD), jnp.bfloat16),
            pltpu.VMEM((2, BLK, HD), jnp.bfloat16),
            pltpu.SMEM((2 * NB,), jnp.int32),
            pltpu.SMEM((2,), jnp.int32),
            pltpu.SemaphoreType.DMA((5,)),
        ],
        compiler_params=params(),
        cost_estimate=cost(2**28, 2**19, 2**21),
        name="window_first",
    )(
        *(far(array) for array in (block_map, window_reach, win_queries, ctx_keyvals, win_keyvals))
    )
    send = pl.pallas_call(
        second_kernel,
        out_shape=shaped((CHIPS, SEND_ROWS, HD), jnp.bfloat16),
        in_specs=[smem] + [vmem] * 6,
        out_specs=vmem,
        scratch_shapes=[pltpu.VMEM((BLK, HEADS * HD), jnp.float32)],
        compiler_params=params(),
        cost_estimate=cost(2**28, 2**19, 2**21),
        name="window_second",
    )(info, queries, sums, tops, totals, ctx_keyvals, other_keyvals)
    got = lax.all_to_all(send, "ctx", 0, 0, axis_index_groups=same_core, tiled=True)
    share = pl.pallas_call(
        combine_kernel,
        out_shape=shaped((CHIPS, SHARE_ROWS, HD), jnp.bfloat16),
        in_specs=[smem, vmem, vmem, vmem],
        out_specs=vmem,
        compiler_params=params(),
        cost_estimate=cost(2**20, 2**12, 2**20),
        name="window_join",
    )(info, got, own_mean, own_level)
    rows_own = lax.all_to_all(share, "ctx", 0, 0, axis_index_groups=same_core, tiled=True)
    rows_other = lax.ppermute(rows_own, "ctx", core_swap)
    shares = pl.pallas_call(
        project_kernel,
        out_shape=shaped((8, 64, BLK), jnp.bfloat16),
        in_specs=[vmem, vmem, vmem],
        out_specs=vmem,
        compiler_params=params(),
        cost_estimate=cost(2**28, 0, 2**21),
        name="project",
    )(rows_own, rows_other, out_weight)
    summands = lax.all_to_all(shares, "tp", 0, 0, tiled=True)
    context_attn = pl.pallas_call(
        block_kernel,
        out_shape=shaped((2 * BLK, HEADS * HD), jnp.bfloat16),
        grid=(2, HEADS // STEP_HEADS),
        in_specs=[
            smem,
            pl.BlockSpec((BLK, STEP_HEADS * HD), lambda slot, step: (slot, step)),
            pl.BlockSpec((2, BLK, HD), lambda slot, step: (0, slot, 0)),
            pl.BlockSpec((CHIPS, SHARE_ROWS, HD), lambda slot, step: (0, 0, 0)),
            pl.BlockSpec((CHIPS, SHARE_ROWS, HD), lambda slot, step: (0, 0, 0)),
        ],
        out_specs=pl.BlockSpec((BLK, STEP_HEADS * HD), lambda slot, step: (slot, step)),
        compiler_params=params(),
        cost_estimate=cost(2**30, 2**21, 2**22),
        name="block_attention",
    )(info, ctx_queries, ctx_keyvals, rows_own, rows_other)
    window_proj = jnp.sum(summands.astype(jnp.float32), axis=0)
    return (context_attn, window_proj)


def solution(mesh):
    return jax.shard_map(
        on_device,
        mesh=mesh,
        in_specs=(
            P("ctx", "tp"),
            P(None, "ctx", "tp"),
            P(),
            P(),
            P(None, None, "tp"),
            P(None, None, None, "tp"),
            P("tp", "ctx"),
        ),
        out_specs=(P("ctx", "tp"), P("tp", "ctx")),
        check_vma=False,
    )
```

```python
import math

import jax
import jax.numpy as jnp
from jax import lax
from jax.experimental import pallas as pl
from jax.experimental.pallas import tpu as pltpu
from jax.sharding import PartitionSpec as P

HD = 128
HEADS = 8
BLK = 256
NB = 32
CHIPS = 16
HALF = 128
STAT = 16
PIECE = 32
SCALE = 1.0 / math.sqrt(HD)
SCALE2 = SCALE * math.log2(math.e)
AHEAD = 2
masked_score = -1e30

SEND_ROWS = HALF + STAT + PIECE
SHARE_ROWS = HALF + PIECE

same_core = [[chip * 2 + core for chip in range(CHIPS)] for core in range(2)]
core_swap = [(device, device ^ 1) for device in range(2 * CHIPS)]

smem = pl.BlockSpec(memory_space=pltpu.SMEM)
vmem = pl.BlockSpec(memory_space=pltpu.VMEM)
hbm = pl.BlockSpec(memory_space=pltpu.HBM)


def params(room=40):
    return pltpu.CompilerParams(vmem_limit_bytes=room * 2**20)


def cost(flops, exps, size):
    return pl.CostEstimate(flops=flops, transcendentals=exps, bytes_accessed=size)


def split_three(value):
    high = value.astype(jnp.bfloat16)
    rest = value - high.astype(jnp.float32)
    middle = rest.astype(jnp.bfloat16)
    low = (rest - middle.astype(jnp.float32)).astype(jnp.bfloat16)
    return high, middle, low


def dot_nt(left, right):
    return lax.dot_general(
        left, right, (((1,), (1,)), ((), ())), preferred_element_type=jnp.float32
    )


def row_softmax(raw):
    top = jnp.max(raw, axis=1, keepdims=True)
    weights = jnp.exp2((raw - top) * SCALE2)
    return top, jnp.sum(weights, axis=1, keepdims=True), weights


def weigh(weights, values):
    return jnp.dot(weights.astype(jnp.bfloat16), values, preferred_element_type=jnp.float32)


def each_head(query_ref, keys):
    ready = []
    for head in range(HEADS + AHEAD):
        if head < HEADS:
            ready.append(dot_nt(query_ref[:, head * HD : (head + 1) * HD], keys))
        if head >= AHEAD:
            yield head - AHEAD, ready.pop(0)


def find_block(map_ref, device, core):
    slot = jnp.where(map_ref[2 * device] // NB == core, 0, 1)
    return slot, map_ref[2 * device + slot] - NB * core


def fetch_kernel(
    map_hbm,
    reach_hbm,
    query_hbm,
    keyval_hbm,
    window_hbm,
    query_ref,
    keyval_ref,
    mean_ref,
    level_ref,
    info_ref,
    window_ref,
    map_ref,
    reach_ref,
    done,
):
    position = lax.axis_index("ctx")
    core = position % 2
    chip = position // 2
    copies = [
        pltpu.make_async_copy(source, target, done.at[number])
        for number, (source, target) in enumerate(
            (
                (map_hbm, map_ref),
                (reach_hbm, reach_ref),
                (query_hbm.at[core], query_ref),
                (window_hbm.at[core], window_ref),
                (keyval_hbm, keyval_ref),
            )
        )
    ]
    for copy in copies:
        copy.start()
    for copy in copies[:2]:
        copy.wait()
    partner = position + 1 - 2 * core
    slot, place = find_block(map_ref, position, core)
    other_slot, other_place = find_block(map_ref, partner, core)
    holder = jnp.int32(0)
    for number in range(2 * NB):
        holder = jnp.where(map_ref[number] == core * NB, number // 4, holder)
    info_ref[0] = holder
    info_ref[1] = jnp.where(place < reach_ref[core], 1, 0)
    info_ref[2] = jnp.where(other_place < reach_ref[core], 1, 0)
    info_ref[3] = place
    info_ref[4] = other_slot
    info_ref[5] = slot
    info_ref[6] = map_ref[2 * position]
    info_ref[7] = map_ref[2 * position + 1]
    for copy in copies[2:]:
        copy.wait()
    half = chip % 2
    query_rows = pl.ds(pl.multiple_of(half * HALF, HALF), HALF)
    query_lanes = pl.ds(pl.multiple_of(chip // 2 * HD, HD), HD)
    raw = dot_nt(query_ref[query_rows, query_lanes], window_ref[0])
    key = lax.broadcasted_iota(jnp.int32, raw.shape, 1)
    row = lax.broadcasted_iota(jnp.int32, raw.shape, 0) + half * HALF
    raw = jnp.where(key <= row, raw, masked_score)
    top, total, weights = row_softmax(raw)
    mean_ref[...] = weigh(weights, window_ref[1]) / total
    level = jnp.broadcast_to(top * SCALE + jnp.log(total), (HALF, HALF)).T
    level_ref[...] = level[:8]


def window_kernel(info_ref, query_ref, own_ref, other_ref, send_ref, sum_ref):
    own_rows = pl.ds(pl.multiple_of(info_ref[5] * BLK, BLK), BLK)
    other_rows = pl.ds(pl.multiple_of(info_ref[4] * BLK, BLK), BLK)
    keys = jnp.concatenate([own_ref[0, own_rows, :], other_ref[0, other_rows, :]], axis=0)
    values = (own_ref[1, own_rows, :], other_ref[1, other_rows, :])
    lane = lax.broadcasted_iota(jnp.int32, (BLK, HD), 1)
    columns = jnp.zeros((BLK, HD), jnp.float32)
    for head, raw in each_head(query_ref, keys):
        for part in range(2):
            top, total, weights = row_softmax(raw[:, part * BLK : (part + 1) * BLK])
            sum_ref[part, :, head * HD : (head + 1) * HD] = weigh(weights, values[part])
            columns = jnp.where(lane == part * HEADS + head, top, columns)
            columns = jnp.where(lane == (2 + part) * HEADS + head, total, columns)
    table = columns.T
    table = [table[number * HEADS : (number + 1) * HEADS] for number in range(4)]
    lives = [info_ref[1 + part] == 1 for part in range(2)]
    tops = [
        jnp.where(live, top * SCALE, masked_score) for live, top in zip(lives, table[:2])
    ]
    joined = jnp.maximum(tops[0], tops[1])
    lifts = [jnp.where(live, jnp.exp(top - joined), 0.0) for live, top in zip(lives, tops)]
    total = table[2] * lifts[0] + table[3] * lifts[1]
    some = total > 0.0
    safe = jnp.where(some, total, 1.0)
    inverse = jnp.where(some, 1.0 / safe, 0.0)
    level = jnp.where(some, joined + jnp.log(safe), masked_score)
    blank = jnp.zeros((HD - 2 * HEADS, BLK), jnp.float32)
    lifts = jnp.concatenate([lifts[0] * inverse, lifts[1] * inverse, blank], axis=0).T
    pieces = [piece.astype(jnp.float32) for piece in split_three(level)]
    row = lax.broadcasted_iota(jnp.int32, (STAT, BLK), 0)
    for head in range(HEADS):
        lanes = slice(head * HD, (head + 1) * HD)
        mean = (
            sum_ref[0, :, lanes] * lifts[:, head : head + 1]
            + sum_ref[1, :, lanes] * lifts[:, HEADS + head : HEADS + head + 1]
        ).astype(jnp.bfloat16)
        stats = jnp.zeros((STAT, BLK), jnp.float32)
        for number, piece in enumerate(pieces):
            stats = jnp.where(row == number, piece[head : head + 1], stats)
        stats = stats.astype(jnp.bfloat16)
        for half in range(2):
            rows = slice(half * HALF, (half + 1) * HALF)
            send_ref[2 * head + half, :HALF, :] = mean[rows]
            send_ref[2 * head + half, HALF : HALF + STAT, :] = stats[:, rows]
    first = info_ref[3] == 0
    for member in range(2):
        block = jnp.where(first, own_ref[member, own_rows, :], other_ref[member, other_rows, :])
        send_ref[8 * member : 8 * member + 8, HALF + STAT :, :] = block.reshape(8, PIECE, HD)


def combine_kernel(info_ref, got_ref, mean_ref, level_ref, share_ref):
    levels = []
    for source in range(CHIPS):
        stats = got_ref[source, HALF : HALF + STAT, :].astype(jnp.float32)
        levels.append(stats[0:1] + stats[1:2] + stats[2:3])
    levels.append(level_ref[0:1, :])
    levels = jnp.concatenate(levels, axis=0)
    lifts = jnp.exp(levels - jnp.max(levels, axis=0, keepdims=True))
    lifts = lifts / jnp.sum(lifts, axis=0, keepdims=True)
    blank = jnp.zeros((HALF - CHIPS - 1, HALF), jnp.float32)
    lifts = jnp.concatenate([lifts, blank], axis=0).T
    joined = mean_ref[...] * lifts[:, CHIPS : CHIPS + 1]
    for source in range(CHIPS):
        part = got_ref[source, :HALF, :].astype(jnp.float32)
        joined = joined + part * lifts[:, source : source + 1]
    result = joined.astype(jnp.bfloat16)
    piece = got_ref[info_ref[0], HALF + STAT :, :]
    for target in range(CHIPS):
        share_ref[target, :HALF, :] = result
        share_ref[target, HALF:, :] = piece


def project_kernel(own_ref, other_ref, weight_ref, out_ref):
    core = lax.axis_index("ctx") % 2
    rows = jnp.concatenate(
        [
            jnp.concatenate([ref[2 * head + half, :HALF, :] for head in range(HEADS)], axis=1)
            for ref in (own_ref, other_ref)
            for half in range(2)
        ],
        axis=0,
    )
    result = jnp.dot(rows, weight_ref[...], preferred_element_type=jnp.float32)
    result = result.reshape(8, 64, BLK).astype(out_ref.dtype)
    out_ref[pl.ds(core * 4, 4)] = result[:4]
    out_ref[pl.ds(4 - core * 4, 4)] = result[4:]


def block_kernel(info_ref, query_ref, keyval_ref, own_ref, other_ref, out_ref):
    core = lax.axis_index("ctx") % 2
    block = info_ref[6 + pl.program_id(0)]
    mine = block // NB == core
    bias = jnp.where(block % NB != 0, 0.0, masked_score)

    def anchor(member):
        taken = slice(8 * member, 8 * member + 8)
        own = own_ref[taken, HALF:, :].reshape(BLK, HD)
        other = other_ref[taken, HALF:, :].reshape(BLK, HD)
        return jnp.where(mine, own, other)

    keys = jnp.concatenate([anchor(0), keyval_ref[0]], axis=0)
    values = jnp.concatenate([anchor(1), keyval_ref[1]], axis=0)
    key = lax.broadcasted_iota(jnp.int32, (BLK, BLK), 1)
    row = lax.broadcasted_iota(jnp.int32, (BLK, BLK), 0)
    live = key <= row
    for head, raw in each_head(query_ref, keys):
        raw = jnp.concatenate(
            [raw[:, :BLK] + bias, jnp.where(live, raw[:, BLK:], masked_score)], axis=1
        )
        _, total, weights = row_softmax(raw)
        result = weigh(weights, values) / total
        out_ref[:, head * HD : (head + 1) * HD] = result.astype(jnp.bfloat16)


def far(array):
    return pltpu.with_memory_space_constraint(array, pltpu.HBM)


def shaped(shape, dtype):
    return jax.ShapeDtypeStruct(shape, dtype)


def on_device(
    ctx_queries, ctx_keyvals, block_map, window_reach, win_queries, win_keyvals, out_weight
):
    other_keyvals = lax.ppermute(ctx_keyvals, "ctx", core_swap)
    queries, keyvals, own_mean, own_level, info = pl.pallas_call(
        fetch_kernel,
        out_shape=(
            shaped((BLK, HEADS * HD), jnp.bfloat16),
            shaped((2, 2 * BLK, HD), jnp.bfloat16),
            shaped((HALF, HD), jnp.float32),
            shaped((8, HALF), jnp.float32),
            shaped((8,), jnp.int32),
        ),
        in_specs=[hbm] * 5,
        out_specs=(vmem,) * 4 + (smem,),
        scratch_shapes=[
            pltpu.VMEM((2, BLK, HD), jnp.bfloat16),
            pltpu.SMEM((2 * NB,), jnp.int32),
            pltpu.SMEM((2,), jnp.int32),
            pltpu.SemaphoreType.DMA((5,)),
        ],
        compiler_params=params(),
        cost_estimate=cost(2**24, 2**15, 2**21),
        name="window_fetch",
    )(
        *(far(array) for array in (block_map, window_reach, win_queries, ctx_keyvals, win_keyvals))
    )
    send = pl.pallas_call(
        window_kernel,
        out_shape=shaped((CHIPS, SEND_ROWS, HD), jnp.bfloat16),
        in_specs=[smem] + [vmem] * 3,
        out_specs=vmem,
        scratch_shapes=[pltpu.VMEM((2, BLK, HEADS * HD), jnp.float32)],
        compiler_params=params(),
        cost_estimate=cost(2**29, 2**20, 2**21),
        name="window_parts",
    )(info, queries, keyvals, other_keyvals)
    got = lax.all_to_all(send, "ctx", 0, 0, axis_index_groups=same_core, tiled=True)
    share = pl.pallas_call(
        combine_kernel,
        out_shape=shaped((CHIPS, SHARE_ROWS, HD), jnp.bfloat16),
        in_specs=[smem, vmem, vmem, vmem],
        out_specs=vmem,
        compiler_params=params(),
        cost_estimate=cost(2**20, 2**12, 2**20),
        name="window_join",
    )(info, got, own_mean, own_level)
    rows_own = lax.all_to_all(share, "ctx", 0, 0, axis_index_groups=same_core, tiled=True)
    rows_other = lax.ppermute(rows_own, "ctx", core_swap)
    shares = pl.pallas_call(
        project_kernel,
        out_shape=shaped((8, 64, BLK), jnp.bfloat16),
        in_specs=[vmem, vmem, vmem],
        out_specs=vmem,
        compiler_params=params(),
        cost_estimate=cost(2**28, 0, 2**21),
        name="project",
    )(rows_own, rows_other, out_weight)
    summands = lax.all_to_all(shares, "tp", 0, 0, tiled=True)
    context_attn = pl.pallas_call(
        block_kernel,
        out_shape=shaped((2 * BLK, HEADS * HD), jnp.bfloat16),
        grid=(2,),
        in_specs=[
            smem,
            pl.BlockSpec((BLK, HEADS * HD), lambda slot: (slot, 0)),
            pl.BlockSpec((2, BLK, HD), lambda slot: (0, slot, 0)),
            pl.BlockSpec((CHIPS, SHARE_ROWS, HD), lambda slot: (0, 0, 0)),
            pl.BlockSpec((CHIPS, SHARE_ROWS, HD), lambda slot: (0, 0, 0)),
        ],
        out_specs=pl.BlockSpec((BLK, HEADS * HD), lambda slot: (slot, 0)),
        compiler_params=params(),
        cost_estimate=cost(2**30, 2**21, 2**22),
        name="block_attention",
    )(info, ctx_queries, ctx_keyvals, rows_own, rows_other)
    window_proj = jnp.sum(summands.astype(jnp.float32), axis=0)
    return (context_attn, window_proj)


def solution(mesh):
    return jax.shard_map(
        on_device,
        mesh=mesh,
        in_specs=(
            P("ctx", "tp"),
            P(None, "ctx", "tp"),
            P(),
            P(),
            P(None, None, "tp"),
            P(None, None, None, "tp"),
            P("tp", "ctx"),
        ),
        out_specs=(P("ctx", "tp"), P("tp", "ctx")),
        check_vma=False,
    )
```

```python
import math

import jax
import jax.numpy as jnp
from jax import lax
from jax.experimental import pallas as pl
from jax.experimental.pallas import tpu as pltpu
from jax.sharding import PartitionSpec as P

HD = 128
HEADS = 8
BLK = 256
NB = 32
CHIPS = 16
HALF = 128
STAT = 16
PIECE = 32
SHARE = 32
SCALE = 1.0 / math.sqrt(HD)
SCALE2 = SCALE * math.log2(math.e)
AHEAD = 2
masked_score = -1e30

SEND_ROWS = HALF + STAT + PIECE
SHARE_ROWS = HALF + PIECE

same_core = [[chip * 2 + core for chip in range(CHIPS)] for core in range(2)]
core_swap = [(device, device ^ 1) for device in range(2 * CHIPS)]

smem = pl.BlockSpec(memory_space=pltpu.SMEM)
vmem = pl.BlockSpec(memory_space=pltpu.VMEM)
hbm = pl.BlockSpec(memory_space=pltpu.HBM)


def params(room=40):
    return pltpu.CompilerParams(vmem_limit_bytes=room * 2**20)


def cost(flops, exps, size):
    return pl.CostEstimate(flops=flops, transcendentals=exps, bytes_accessed=size)


def split_three(value):
    high = value.astype(jnp.bfloat16)
    rest = value - high.astype(jnp.float32)
    middle = rest.astype(jnp.bfloat16)
    low = (rest - middle.astype(jnp.float32)).astype(jnp.bfloat16)
    return high, middle, low


def dot_nt(left, right):
    return lax.dot_general(
        left, right, (((1,), (1,)), ((), ())), preferred_element_type=jnp.float32
    )


def row_softmax(raw):
    top = jnp.max(raw, axis=1, keepdims=True)
    weights = jnp.exp2((raw - top) * SCALE2)
    return top, jnp.sum(weights, axis=1, keepdims=True), weights


def weigh(weights, values):
    return jnp.dot(weights.astype(jnp.bfloat16), values, preferred_element_type=jnp.float32)


def each_head(query_ref, keys):
    ready = []
    for head in range(HEADS + AHEAD):
        if head < HEADS:
            ready.append(dot_nt(query_ref[:, head * HD : (head + 1) * HD], keys))
        if head >= AHEAD:
            yield head - AHEAD, ready.pop(0)


def fetch_kernel(
    map_hbm,
    reach_hbm,
    query_hbm,
    keyval_hbm,
    window_hbm,
    query_ref,
    keyval_ref,
    mean_ref,
    level_ref,
    info_ref,
    window_ref,
    map_ref,
    reach_ref,
    done,
):
    position = lax.axis_index("ctx")
    core = position % 2
    chip = position // 2
    copies = [
        pltpu.make_async_copy(source, target, done.at[number])
        for number, (source, target) in enumerate(
            (
                (map_hbm, map_ref),
                (reach_hbm, reach_ref),
                (query_hbm.at[:, :, core], query_ref),
                (window_hbm.at[chip % 2], window_ref),
                (keyval_hbm, keyval_ref),
            )
        )
    ]
    for copy in copies:
        copy.start()
    for copy in copies[:2]:
        copy.wait()
    partner = position + 1 - 2 * core
    holder = jnp.int32(0)
    for number in range(2 * NB):
        holder = jnp.where(map_ref[number] == core * NB, number // 4, holder)
    info_ref[0] = holder
    for part, device in enumerate((position, partner)):
        info_ref[1 + part] = jnp.where(map_ref[2 * device] // NB == 0, 0, 1)
        for context in range(2):
            slot = jnp.where(map_ref[2 * device] // NB == context, 0, 1)
            place = map_ref[2 * device + slot] - NB * context
            info_ref[3 + 2 * context + part] = jnp.where(place < reach_ref[context], 1, 0)
    slot = jnp.where(map_ref[2 * position] // NB == core, 0, 1)
    info_ref[7] = map_ref[2 * position + slot] - NB * core
    info_ref[8] = core
    info_ref[9] = map_ref[2 * position]
    info_ref[10] = map_ref[2 * position + 1]
    for copy in copies[2:]:
        copy.wait()
    lanes = pl.ds(pl.multiple_of(chip // 2 * HD, HD), HD)
    query = query_ref[chip % 2, :, :, lanes].reshape(HALF, HD)
    raw = dot_nt(query, window_ref[0])
    key = lax.broadcasted_iota(jnp.int32, raw.shape, 1)
    row = lax.broadcasted_iota(jnp.int32, raw.shape, 0)
    row = row // SHARE * (2 * SHARE) + core * SHARE + row % SHARE
    raw = jnp.where(key <= row, raw, masked_score)
    top, total, weights = row_softmax(raw)
    mean_ref[...] = weigh(weights, window_ref[1]) / total
    level = jnp.broadcast_to(top * SCALE + jnp.log(total), (HALF, HALF)).T
    level_ref[...] = level[:8]


def window_kernel(
    info_ref,
    query_ref,
    own_ref,
    other_ref,
    rows_hbm,
    send_ref,
    score_hbm,
    score_ref,
    rows_ref,
    done,
):
    copy = pltpu.make_async_copy(rows_hbm.at[:BLK], rows_ref, done.at[0])

    @pl.when(info_ref[8] == 0)
    def _():
        copy.start()

    def block_rows(part, context):
        slot = info_ref[1 + part]
        slot = slot if context == 0 else 1 - slot
        return pl.ds(pl.multiple_of(slot * BLK, BLK), BLK)

    sources = (own_ref, other_ref)
    lane = lax.broadcasted_iota(jnp.int32, (BLK, HD), 1)
    columns = jnp.zeros((BLK, HD), jnp.float32)
    steps = [(context, pair) for context in range(2) for pair in range(HEADS // 2)]
    keys = []
    values = []
    biases = []
    for context in range(2):
        rows = [block_rows(part, context) for part in range(2)]
        keys.append(
            jnp.concatenate([ref[0, taken, :] for ref, taken in zip(sources, rows)], axis=0)
        )
        values.append([ref[1, taken, :] for ref, taken in zip(sources, rows)])
        biases.append(
            [
                jnp.where(info_ref[3 + 2 * context + part] == 1, 0.0, masked_score)
                for part in range(2)
            ]
        )

    def score(step):
        context, pair = steps[step]
        query = jnp.concatenate(
            [
                query_ref[context, :, :, head * HD : (head + 1) * HD].reshape(HALF, HD)
                for head in (2 * pair, 2 * pair + 1)
            ],
            axis=0,
        )
        return dot_nt(query, keys[context])

    ready = [score(step) for step in range(AHEAD)]
    for step, (context, pair) in enumerate(steps):
        if step + AHEAD < len(steps):
            ready.append(score(step + AHEAD))
        raw = ready.pop(0)
        parts = []
        for part in range(2):
            top, total, weights = row_softmax(raw[:, part * BLK : (part + 1) * BLK])
            parts.append(
                (top + biases[context][part], total, weigh(weights, values[context][part]))
            )
        joined = jnp.maximum(parts[0][0], parts[1][0])
        lifts = [jnp.exp2((part[0] - joined) * SCALE2) for part in parts]
        total = parts[0][1] * lifts[0] + parts[1][1] * lifts[1]
        inverse = 1.0 / total
        mean = parts[0][2] * (lifts[0] * inverse) + parts[1][2] * (lifts[1] * inverse)
        mean = mean.astype(jnp.bfloat16)
        for half in range(2):
            target = 2 * (2 * pair + half) + context
            send_ref[target, :HALF, :] = mean[half * HALF : (half + 1) * HALF]
        columns = jnp.where(lane == step, joined, columns)
        columns = jnp.where(lane == len(steps) + step, total, columns)
    table = columns.T
    level = table[:HEADS] * SCALE + jnp.log(table[HEADS : 2 * HEADS])
    pieces = [piece.astype(jnp.float32) for piece in split_three(level)]
    row = lax.broadcasted_iota(jnp.int32, (STAT, BLK), 0)
    for step, (context, pair) in enumerate(steps):
        stats = jnp.zeros((STAT, BLK), jnp.float32)
        for number, piece in enumerate(pieces):
            stats = jnp.where(row == number, piece[step : step + 1], stats)
        stats = stats.astype(jnp.bfloat16)
        for half in range(2):
            target = 2 * (2 * pair + half) + context
            lanes = slice(half * HALF, (half + 1) * HALF)
            send_ref[target, HALF : HALF + STAT, :] = stats[:, lanes]
    first = info_ref[7] == 0
    own_rows, other_rows = [
        pl.ds(pl.multiple_of((info_ref[1 + part] ^ info_ref[8]) * BLK, BLK), BLK)
        for part in range(2)
    ]
    for member in range(2):
        block = jnp.where(first, own_ref[member, own_rows, :], other_ref[member, other_rows, :])
        send_ref[8 * member : 8 * member + 8, HALF + STAT :, :] = block.reshape(8, PIECE, HD)

    @pl.when(info_ref[8] == 0)
    def _():
        copy.wait()
        for head in range(HEADS):
            query = rows_ref[:, head * HD : (head + 1) * HD]
            score_ref[head] = dot_nt(query, own_ref[0, :BLK, :])
        copy_out = pltpu.make_async_copy(score_ref, score_hbm, done.at[1])
        copy_out.start()
        copy_out.wait()


def combine_kernel(info_ref, got_ref, mean_ref, level_ref, share_ref):
    levels = []
    for source in range(CHIPS):
        stats = got_ref[source, HALF : HALF + STAT, :].astype(jnp.float32)
        levels.append(stats[0:1] + stats[1:2] + stats[2:3])
    levels.append(level_ref[0:1, :])
    levels = jnp.concatenate(levels, axis=0)
    lifts = jnp.exp(levels - jnp.max(levels, axis=0, keepdims=True))
    lifts = lifts / jnp.sum(lifts, axis=0, keepdims=True)
    count = 3 * (CHIPS + 1)
    source_of = lax.broadcasted_iota(jnp.int32, (count, (CHIPS + 1) * HALF), 0) % (CHIPS + 1)
    column = lax.broadcasted_iota(jnp.int32, (count, (CHIPS + 1) * HALF), 1) // HALF
    spread = jnp.where(source_of == column, 1.0, 0.0).astype(jnp.bfloat16)
    wide = lax.dot_general(
        jnp.concatenate(split_three(lifts), axis=0),
        spread,
        (((0,), (0,)), ((), ())),
        preferred_element_type=jnp.float32,
    )
    joined = mean_ref[...] * wide[:, CHIPS * HALF :]
    for source in range(CHIPS):
        part = got_ref[source, :HALF, :].astype(jnp.float32)
        joined = joined + part * wide[:, source * HALF : (source + 1) * HALF]
    result = joined.astype(jnp.bfloat16)
    piece = got_ref[info_ref[0], HALF + STAT :, :]
    for target in range(CHIPS):
        share_ref[target, :HALF, :] = result
        share_ref[target, HALF:, :] = piece


def project_kernel(rows_ref, own_ref, other_ref, out_ref, anchor_ref):
    rows = jnp.concatenate(
        [
            jnp.concatenate(
                [rows_ref[2 * head + context, :HALF, :] for head in range(HEADS)], axis=1
            )
            for context in range(2)
        ],
        axis=0,
    )
    core = lax.axis_index("ctx") % 2

    def fill(weights):
        for number, ref in enumerate(weights):
            result = jnp.dot(rows, ref[...], preferred_element_type=jnp.float32)
            lanes = slice(number * BLK, (number + 1) * BLK)
            out_ref[:, :, lanes] = result.reshape(8, SHARE, BLK).astype(out_ref.dtype)

    @pl.when(core == 0)
    def _():
        fill((own_ref, other_ref))

    @pl.when(core == 1)
    def _():
        fill((other_ref, own_ref))

    anchor_ref[...] = rows_ref[:, HALF:, :].reshape(2, BLK, HD)


def total_kernel(parts_ref, mine_ref, theirs_ref):
    core = lax.axis_index("ctx") % 2
    for number in range(2):
        lanes = slice(number * BLK, (number + 1) * BLK)
        total = parts_ref[0, :, lanes].astype(jnp.float32)
        for plane in range(1, 8):
            total = total + parts_ref[plane, :, lanes].astype(jnp.float32)

        @pl.when(core == number)
        def _(total=total):
            mine_ref[...] = total

        @pl.when(core != number)
        def _(total=total):
            theirs_ref[...] = total


def block_kernel(
    info_ref, query_ref, keyval_ref, own_ref, other_ref, score_hbm, out_ref, score_ref, done
):
    step = pl.program_id(0)
    scored = (step == 1) & (info_ref[8] == 0)
    block = info_ref[10 - step]
    copy = pltpu.make_async_copy(score_hbm, score_ref, done)

    @pl.when((step == 0) & (info_ref[8] == 0))
    def _():
        copy.start()

    mine = block // NB == info_ref[8]
    bias = jnp.where(block % NB != 0, 0.0, masked_score)

    def anchor(member):
        return jnp.where(mine, own_ref[member], other_ref[member])

    values = jnp.concatenate([anchor(1), keyval_ref[1]], axis=0)
    key = lax.broadcasted_iota(jnp.int32, (BLK, BLK), 1)
    row = lax.broadcasted_iota(jnp.int32, (BLK, BLK), 0)
    live = key <= row

    def finish(head, former, latter):
        raw = jnp.concatenate([former + bias, jnp.where(live, latter, masked_score)], axis=1)
        _, total, weights = row_softmax(raw)
        result = weigh(weights, values) / total
        out_ref[:, head * HD : (head + 1) * HD] = result.astype(jnp.bfloat16)

    @pl.when(scored)
    def _():
        copy.wait()
        for head, raw in each_head(query_ref, anchor(0)):
            finish(head, raw, score_ref[head])

    @pl.when(jnp.logical_not(scored))
    def _():
        keys = jnp.concatenate([anchor(0), keyval_ref[0]], axis=0)
        for head, raw in each_head(query_ref, keys):
            finish(head, raw[:, :BLK], raw[:, BLK:])


def far(array):
    return pltpu.with_memory_space_constraint(array, pltpu.HBM)


def shaped(shape, dtype):
    return jax.ShapeDtypeStruct(shape, dtype)


def on_device(
    ctx_queries, ctx_keyvals, block_map, window_reach, win_queries, win_keyvals, out_weight
):
    other_keyvals = lax.ppermute(ctx_keyvals, "ctx", core_swap)
    halves = win_queries.reshape(2, 4, 2, SHARE, HEADS * HD)
    queries, keyvals, own_mean, own_level, info = pl.pallas_call(
        fetch_kernel,
        out_shape=(
            shaped((2, 4, SHARE, HEADS * HD), jnp.bfloat16),
            shaped((2, 2 * BLK, HD), jnp.bfloat16),
            shaped((HALF, HD), jnp.float32),
            shaped((8, HALF), jnp.float32),
            shaped((16,), jnp.int32),
        ),
        in_specs=[hbm] * 5,
        out_specs=(vmem,) * 4 + (smem,),
        scratch_shapes=[
            pltpu.VMEM((2, BLK, HD), jnp.bfloat16),
            pltpu.SMEM((2 * NB,), jnp.int32),
            pltpu.SMEM((2,), jnp.int32),
            pltpu.SemaphoreType.DMA((5,)),
        ],
        compiler_params=params(),
        cost_estimate=cost(2**24, 2**15, 2**21),
        name="window_fetch",
    )(
        *(far(array) for array in (block_map, window_reach, halves, ctx_keyvals, win_keyvals))
    )
    queries, other_keyvals, out_weight = lax.optimization_barrier(
        (queries, other_keyvals, out_weight)
    )
    other_weight = lax.ppermute(out_weight, "ctx", core_swap)
    send, scores = pl.pallas_call(
        window_kernel,
        out_shape=(
            shaped((CHIPS, SEND_ROWS, HD), jnp.bfloat16),
            pltpu.HBM((HEADS, BLK, BLK), jnp.float32),
        ),
        in_specs=[smem] + [vmem] * 3 + [hbm],
        out_specs=(vmem, hbm),
        scratch_shapes=[
            pltpu.VMEM((HEADS, BLK, BLK), jnp.float32),
            pltpu.VMEM((BLK, HEADS * HD), jnp.bfloat16),
            pltpu.SemaphoreType.DMA((2,)),
        ],
        compiler_params=params(),
        cost_estimate=cost(2**29, 2**20, 2**21),
        name="window_parts",
    )(info, queries, keyvals, other_keyvals, far(ctx_queries))
    send, other_weight = lax.optimization_barrier((send, other_weight))
    got = lax.all_to_all(send, "ctx", 0, 0, axis_index_groups=same_core, tiled=True)
    share = pl.pallas_call(
        combine_kernel,
        out_shape=shaped((CHIPS, SHARE_ROWS, HD), jnp.bfloat16),
        in_specs=[smem, vmem, vmem, vmem],
        out_specs=vmem,
        compiler_params=params(),
        cost_estimate=cost(2**20, 2**12, 2**20),
        name="window_join",
    )(info, got, own_mean, own_level)
    rows = lax.all_to_all(share, "ctx", 0, 0, axis_index_groups=same_core, tiled=True)
    shares, anchor = pl.pallas_call(
        project_kernel,
        out_shape=(
            shaped((8, SHARE, 2 * BLK), jnp.bfloat16),
            shaped((2, BLK, HD), jnp.bfloat16),
        ),
        in_specs=[vmem, vmem, vmem],
        out_specs=(vmem, vmem),
        compiler_params=params(),
        cost_estimate=cost(2**28, 0, 2**21),
        name="project",
    )(rows, out_weight, other_weight)
    summands = lax.all_to_all(shares, "tp", 0, 0, tiled=True)
    other_anchor = lax.ppermute(anchor, "ctx", core_swap)
    context_attn = pl.pallas_call(
        block_kernel,
        out_shape=shaped((2 * BLK, HEADS * HD), jnp.bfloat16),
        grid=(2,),
        in_specs=[
            smem,
            pl.BlockSpec((BLK, HEADS * HD), lambda step: (1 - step, 0)),
            pl.BlockSpec((2, BLK, HD), lambda step: (0, 1 - step, 0)),
            pl.BlockSpec((2, BLK, HD), lambda step: (0, 0, 0)),
            pl.BlockSpec((2, BLK, HD), lambda step: (0, 0, 0)),
            hbm,
        ],
        out_specs=pl.BlockSpec((BLK, HEADS * HD), lambda step: (1 - step, 0)),
        scratch_shapes=[
            pltpu.VMEM((HEADS, BLK, BLK), jnp.float32),
            pltpu.SemaphoreType.DMA,
        ],
        compiler_params=params(),
        cost_estimate=cost(2**30, 2**21, 2**22),
        name="block_attention",
    )(info, ctx_queries, ctx_keyvals, anchor, other_anchor, far(scores))
    summands, context_attn = lax.optimization_barrier((summands, context_attn))
    half_shape = shaped((SHARE, BLK), jnp.float32)
    mine, theirs = pl.pallas_call(
        total_kernel,
        out_shape=(half_shape, half_shape),
        in_specs=[vmem],
        out_specs=(vmem, vmem),
        compiler_params=params(),
        name="plane_sum",
    )(summands)
    theirs = lax.ppermute(theirs, "ctx", core_swap)
    even = lax.axis_index("ctx") % 2 == 0
    window_proj = jnp.concatenate(
        [jnp.where(even, mine, theirs), jnp.where(even, theirs, mine)], axis=0
    )
    return (context_attn, window_proj)


def solution(mesh):
    return jax.shard_map(
        on_device,
        mesh=mesh,
        in_specs=(
            P("ctx", "tp"),
            P(None, "ctx", "tp"),
            P(),
            P(),
            P(None, None, "tp"),
            P(None, None, None, "tp"),
            P("tp", "ctx"),
        ),
        out_specs=(P("ctx", "tp"), P("tp", "ctx")),
        check_vma=False,
    )
```

```python
import math

import jax
import jax.numpy as jnp
from jax import lax
from jax.experimental import pallas as pl
from jax.experimental.pallas import tpu as pltpu
from jax.sharding import PartitionSpec as P

HD = 128
HEADS = 8
BLK = 256
NB = 32
CHIPS = 16
HALF = 128
STAT = 16
PIECE = 32
SHARE = 32
SCALE = 1.0 / math.sqrt(HD)
SCALE2 = SCALE * math.log2(math.e)
AHEAD = 2
masked_score = -1e30

SEND_ROWS = HALF + STAT + PIECE
SHARE_ROWS = HALF + PIECE

same_core = [[chip * 2 + core for chip in range(CHIPS)] for core in range(2)]
core_swap = [(device, device ^ 1) for device in range(2 * CHIPS)]

vmem = pl.BlockSpec(memory_space=pltpu.VMEM)
hbm = pl.BlockSpec(memory_space=pltpu.HBM)


def params(room=40):
    return pltpu.CompilerParams(vmem_limit_bytes=room * 2**20)


def cost(flops, exps, size):
    return pl.CostEstimate(flops=flops, transcendentals=exps, bytes_accessed=size)


def split_three(value):
    high = value.astype(jnp.bfloat16)
    rest = value - high.astype(jnp.float32)
    middle = rest.astype(jnp.bfloat16)
    low = (rest - middle.astype(jnp.float32)).astype(jnp.bfloat16)
    return high, middle, low


def dot_nt(left, right):
    return lax.dot_general(
        left, right, (((1,), (1,)), ((), ())), preferred_element_type=jnp.float32
    )


def row_softmax(raw):
    top = jnp.max(raw, axis=1, keepdims=True)
    weights = jnp.exp2((raw - top) * SCALE2)
    return top, jnp.sum(weights, axis=1, keepdims=True), weights


def weigh(weights, values):
    return jnp.dot(weights.astype(jnp.bfloat16), values, preferred_element_type=jnp.float32)


def each_head(query_ref, keys):
    ready = []
    for head in range(HEADS + AHEAD):
        if head < HEADS:
            ready.append(dot_nt(query_ref[:, head * HD : (head + 1) * HD], keys))
        if head >= AHEAD:
            yield head - AHEAD, ready.pop(0)


def read(info_ref, number):
    return jnp.max(info_ref[number : number + 1, :]).astype(jnp.int32)


def own_window(query_ref, window_ref):
    position = lax.axis_index("ctx")
    core = position % 2
    chip = position // 2
    lanes = pl.ds(pl.multiple_of(chip // 2 * HD, HD), HD)
    query = query_ref[chip % 2, :, :, lanes].reshape(HALF, HD)
    raw = dot_nt(query, window_ref[0])
    key = lax.broadcasted_iota(jnp.int32, raw.shape, 1)
    row = lax.broadcasted_iota(jnp.int32, raw.shape, 0)
    row = row // SHARE * (2 * SHARE) + core * SHARE + row % SHARE
    raw = jnp.where(key <= row, raw, masked_score)
    top, total, weights = row_softmax(raw)
    mean = weigh(weights, window_ref[1]) / total
    level = jnp.broadcast_to(top * SCALE + jnp.log(total), (HALF, HALF)).T
    return mean, level[:8]


def fetch_kernel(
    map_hbm,
    reach_hbm,
    query_hbm,
    keyval_hbm,
    window_hbm,
    query_ref,
    keyval_ref,
    window_ref,
    info_ref,
    map_ref,
    reach_ref,
    done,
):
    position = lax.axis_index("ctx")
    core = position % 2
    chip = position // 2
    copies = [
        pltpu.make_async_copy(source, target, done.at[number])
        for number, (source, target) in enumerate(
            (
                (map_hbm, map_ref),
                (reach_hbm, reach_ref),
                (query_hbm.at[:, :, core], query_ref),
                (keyval_hbm, keyval_ref),
                (window_hbm.at[chip % 2], window_ref),
            )
        )
    ]
    for copy in copies:
        copy.start()
    for copy in copies[:2]:
        copy.wait()
    partner = position + 1 - 2 * core

    def put(number, value):
        info_ref[number : number + 1, :] = jnp.full((1, HD), value.astype(jnp.float32))

    holder = jnp.int32(0)
    for number in range(2 * NB):
        holder = jnp.where(map_ref[number] == core * NB, number // 4, holder)
    put(0, holder)
    for part, device in enumerate((position, partner)):
        put(1 + part, map_ref[2 * device] // NB)
        for context in range(2):
            slot = jnp.where(map_ref[2 * device] // NB == context, 0, 1)
            place = map_ref[2 * device + slot] - NB * context
            put(3 + 2 * context + part, jnp.where(place < reach_ref[context], 1, 0))
    slot = jnp.where(map_ref[2 * position] // NB == core, 0, 1)
    put(7, map_ref[2 * position + slot] - NB * core)
    put(8, map_ref[2 * position])
    put(9, map_ref[2 * position + 1])
    for copy in copies[2:]:
        copy.wait()


def window_kernel(
    info_ref,
    query_ref,
    own_ref,
    other_ref,
    window_ref,
    rows_hbm,
    send_ref,
    mean_ref,
    level_ref,
    score_hbm,
    score_ref,
    rows_ref,
    done,
):
    core = lax.axis_index("ctx") % 2
    copy = pltpu.make_async_copy(rows_hbm.at[:BLK], rows_ref, done.at[0])

    @pl.when(core == 0)
    def _():
        copy.start()

    slots = [read(info_ref, 1 + part) for part in range(2)]

    def block_rows(part, context):
        slot = slots[part] if context == 0 else 1 - slots[part]
        return pl.ds(pl.multiple_of(slot * BLK, BLK), BLK)

    sources = (own_ref, other_ref)
    lane = lax.broadcasted_iota(jnp.int32, (BLK, HD), 1)
    columns = jnp.zeros((BLK, HD), jnp.float32)
    steps = [(context, pair) for context in range(2) for pair in range(HEADS // 2)]
    keys = []
    values = []
    biases = []
    for context in range(2):
        rows = [block_rows(part, context) for part in range(2)]
        keys.append(
            jnp.concatenate([ref[0, taken, :] for ref, taken in zip(sources, rows)], axis=0)
        )
        values.append([ref[1, taken, :] for ref, taken in zip(sources, rows)])
        biases.append(
            [
                jnp.where(read(info_ref, number) == 1, 0.0, masked_score)
                for number in (3 + 2 * context, 4 + 2 * context)
            ]
        )

    def score(step):
        context, pair = steps[step]
        query = jnp.concatenate(
            [
                query_ref[context, :, :, head * HD : (head + 1) * HD].reshape(HALF, HD)
                for head in (2 * pair, 2 * pair + 1)
            ],
            axis=0,
        )
        return dot_nt(query, keys[context])

    ready = [score(step) for step in range(AHEAD)]
    for step, (context, pair) in enumerate(steps):
        if step + AHEAD < len(steps):
            ready.append(score(step + AHEAD))
        raw = ready.pop(0)
        parts = []
        for part in range(2):
            top, total, weights = row_softmax(raw[:, part * BLK : (part + 1) * BLK])
            parts.append(
                (top + biases[context][part], total, weigh(weights, values[context][part]))
            )
        joined = jnp.maximum(parts[0][0], parts[1][0])
        lifts = [jnp.exp2((part[0] - joined) * SCALE2) for part in parts]
        total = parts[0][1] * lifts[0] + parts[1][1] * lifts[1]
        inverse = 1.0 / total
        mean = parts[0][2] * (lifts[0] * inverse) + parts[1][2] * (lifts[1] * inverse)
        mean = mean.astype(jnp.bfloat16)
        for half in range(2):
            target = 2 * (2 * pair + half) + context
            send_ref[target, :HALF, :] = mean[half * HALF : (half + 1) * HALF]
        columns = jnp.where(lane == step, joined, columns)
        columns = jnp.where(lane == len(steps) + step, total, columns)
    table = columns.T
    level = table[:HEADS] * SCALE + jnp.log(table[HEADS : 2 * HEADS])
    pieces = [piece.astype(jnp.float32) for piece in split_three(level)]
    row = lax.broadcasted_iota(jnp.int32, (STAT, BLK), 0)
    for step, (context, pair) in enumerate(steps):
        stats = jnp.zeros((STAT, BLK), jnp.float32)
        for number, piece in enumerate(pieces):
            stats = jnp.where(row == number, piece[step : step + 1], stats)
        stats = stats.astype(jnp.bfloat16)
        for half in range(2):
            target = 2 * (2 * pair + half) + context
            lanes = slice(half * HALF, (half + 1) * HALF)
            send_ref[target, HALF : HALF + STAT, :] = stats[:, lanes]
    first = read(info_ref, 7) == 0
    own_rows, other_rows = [
        pl.ds(pl.multiple_of((slots[part] ^ core) * BLK, BLK), BLK) for part in range(2)
    ]
    for member in range(2):
        block = jnp.where(first, own_ref[member, own_rows, :], other_ref[member, other_rows, :])
        send_ref[8 * member : 8 * member + 8, HALF + STAT :, :] = block.reshape(8, PIECE, HD)

    @pl.when(core == 0)
    def _():
        mean_ref[...], level_ref[...] = own_window(query_ref, window_ref)
        copy.wait()
        for head in range(HEADS):
            query = rows_ref[:, head * HD : (head + 1) * HD]
            score_ref[head] = dot_nt(query, own_ref[0, :BLK, :])
        copy_out = pltpu.make_async_copy(score_ref, score_hbm, done.at[1])
        copy_out.start()
        copy_out.wait()


def combine_kernel(
    info_ref, got_ref, mean_in, level_in, query_ref, window_ref, share_ref, mean_ref, level_ref
):
    core = lax.axis_index("ctx") % 2

    @pl.when(core == 0)
    def _():
        mean_ref[...] = mean_in[...]
        level_ref[...] = level_in[...]

    @pl.when(core == 1)
    def _():
        mean_ref[...], level_ref[...] = own_window(query_ref, window_ref)

    levels = []
    for source in range(CHIPS):
        stats = got_ref[source, HALF : HALF + STAT, :].astype(jnp.float32)
        levels.append(stats[0:1] + stats[1:2] + stats[2:3])
    levels.append(level_ref[0:1, :])
    levels = jnp.concatenate(levels, axis=0)
    lifts = jnp.exp(levels - jnp.max(levels, axis=0, keepdims=True))
    lifts = lifts / jnp.sum(lifts, axis=0, keepdims=True)
    count = 3 * (CHIPS + 1)
    source_of = lax.broadcasted_iota(jnp.int32, (count, (CHIPS + 1) * HALF), 0) % (CHIPS + 1)
    column = lax.broadcasted_iota(jnp.int32, (count, (CHIPS + 1) * HALF), 1) // HALF
    spread = jnp.where(source_of == column, 1.0, 0.0).astype(jnp.bfloat16)
    wide = lax.dot_general(
        jnp.concatenate(split_three(lifts), axis=0),
        spread,
        (((0,), (0,)), ((), ())),
        preferred_element_type=jnp.float32,
    )
    joined = mean_ref[...] * wide[:, CHIPS * HALF :]
    for source in range(CHIPS):
        part = got_ref[source, :HALF, :].astype(jnp.float32)
        joined = joined + part * wide[:, source * HALF : (source + 1) * HALF]
    result = joined.astype(jnp.bfloat16)
    piece = got_ref[read(info_ref, 0), HALF + STAT :, :]
    for target in range(CHIPS):
        share_ref[target, :HALF, :] = result
        share_ref[target, HALF:, :] = piece


def project_kernel(rows_ref, own_ref, other_ref, out_ref, anchor_ref):
    rows = jnp.concatenate(
        [
            jnp.concatenate(
                [rows_ref[2 * head + context, :HALF, :] for head in range(HEADS)], axis=1
            )
            for context in range(2)
        ],
        axis=0,
    )
    core = lax.axis_index("ctx") % 2

    def fill(weights):
        for number, ref in enumerate(weights):
            result = jnp.dot(rows, ref[...], preferred_element_type=jnp.float32)
            lanes = slice(number * BLK, (number + 1) * BLK)
            out_ref[:, :, lanes] = result.reshape(8, SHARE, BLK).astype(out_ref.dtype)

    @pl.when(core == 0)
    def _():
        fill((own_ref, other_ref))

    @pl.when(core == 1)
    def _():
        fill((other_ref, own_ref))

    anchor_ref[...] = rows_ref[:, HALF:, :].reshape(2, BLK, HD)


def total_kernel(parts_ref, mine_ref, theirs_ref):
    core = lax.axis_index("ctx") % 2
    for number in range(2):
        lanes = slice(number * BLK, (number + 1) * BLK)
        total = parts_ref[0, :, lanes].astype(jnp.float32)
        for plane in range(1, 8):
            total = total + parts_ref[plane, :, lanes].astype(jnp.float32)

        @pl.when(core == number)
        def _(total=total):
            mine_ref[...] = total

        @pl.when(core != number)
        def _(total=total):
            theirs_ref[...] = total


def block_kernel(
    info_ref, query_ref, keyval_ref, own_ref, other_ref, score_hbm, out_ref, score_ref, done
):
    step = pl.program_id(0)
    core = lax.axis_index("ctx") % 2
    scored = (step == 1) & (core == 0)
    block = jnp.where(step == 0, read(info_ref, 9), read(info_ref, 8))
    mine = block // NB == core
    bias = jnp.where(block % NB != 0, 0.0, masked_score)
    copy = pltpu.make_async_copy(score_hbm, score_ref, done)

    @pl.when((step == 0) & (core == 0))
    def _():
        copy.start()


    def anchor(member):
        return jnp.where(mine, own_ref[member], other_ref[member])

    values = jnp.concatenate([anchor(1), keyval_ref[1]], axis=0)
    key = lax.broadcasted_iota(jnp.int32, (BLK, BLK), 1)
    row = lax.broadcasted_iota(jnp.int32, (BLK, BLK), 0)
    live = key <= row

    def finish(head, former, latter):
        raw = jnp.concatenate([former + bias, jnp.where(live, latter, masked_score)], axis=1)
        _, total, weights = row_softmax(raw)
        result = weigh(weights, values) / total
        out_ref[:, head * HD : (head + 1) * HD] = result.astype(jnp.bfloat16)

    @pl.when(scored)
    def _():
        copy.wait()
        for head, raw in each_head(query_ref, anchor(0)):
            finish(head, raw, score_ref[head])

    @pl.when(jnp.logical_not(scored))
    def _():
        keys = jnp.concatenate([anchor(0), keyval_ref[0]], axis=0)
        for head, raw in each_head(query_ref, keys):
            finish(head, raw[:, :BLK], raw[:, BLK:])


def far(array):
    return pltpu.with_memory_space_constraint(array, pltpu.HBM)


def shaped(shape, dtype):
    return jax.ShapeDtypeStruct(shape, dtype)


def on_device(
    ctx_queries, ctx_keyvals, block_map, window_reach, win_queries, win_keyvals, out_weight
):
    other_keyvals = lax.ppermute(ctx_keyvals, "ctx", core_swap)
    halves = win_queries.reshape(2, 4, 2, SHARE, HEADS * HD)
    queries, keyvals, window, info = pl.pallas_call(
        fetch_kernel,
        out_shape=(
            shaped((2, 4, SHARE, HEADS * HD), jnp.bfloat16),
            shaped((2, 2 * BLK, HD), jnp.bfloat16),
            shaped((2, BLK, HD), jnp.bfloat16),
            shaped((16, HD), jnp.float32),
        ),
        in_specs=[hbm] * 5,
        out_specs=(vmem,) * 4,
        scratch_shapes=[
            pltpu.SMEM((2 * NB,), jnp.int32),
            pltpu.SMEM((2,), jnp.int32),
            pltpu.SemaphoreType.DMA((5,)),
        ],
        compiler_params=params(),
        cost_estimate=cost(2**24, 2**15, 2**21),
        name="window_fetch",
    )(
        *(far(array) for array in (block_map, window_reach, halves, ctx_keyvals, win_keyvals))
    )
    queries, other_keyvals, out_weight = lax.optimization_barrier(
        (queries, other_keyvals, out_weight)
    )
    other_weight = lax.ppermute(out_weight, "ctx", core_swap)
    send, own_mean, own_level, scores = pl.pallas_call(
        window_kernel,
        out_shape=(
            shaped((CHIPS, SEND_ROWS, HD), jnp.bfloat16),
            shaped((HALF, HD), jnp.float32),
            shaped((8, HALF), jnp.float32),
            pltpu.HBM((HEADS, BLK, BLK), jnp.float32),
        ),
        in_specs=[vmem] * 5 + [hbm],
        out_specs=(vmem, vmem, vmem, hbm),
        scratch_shapes=[
            pltpu.VMEM((HEADS, BLK, BLK), jnp.float32),
            pltpu.VMEM((BLK, HEADS * HD), jnp.bfloat16),
            pltpu.SemaphoreType.DMA((2,)),
        ],
        compiler_params=params(),
        cost_estimate=cost(2**29, 2**20, 2**21),
        name="window_parts",
    )(info, queries, keyvals, other_keyvals, window, far(ctx_queries))
    send, other_weight = lax.optimization_barrier((send, other_weight))
    got = lax.all_to_all(send, "ctx", 0, 0, axis_index_groups=same_core, tiled=True)
    share = pl.pallas_call(
        combine_kernel,
        out_shape=shaped((CHIPS, SHARE_ROWS, HD), jnp.bfloat16),
        in_specs=[vmem] * 6,
        out_specs=vmem,
        scratch_shapes=[
            pltpu.VMEM((HALF, HD), jnp.float32),
            pltpu.VMEM((8, HALF), jnp.float32),
        ],
        compiler_params=params(),
        cost_estimate=cost(2**20, 2**12, 2**20),
        name="window_join",
    )(info, got, own_mean, own_level, queries, window)
    rows = lax.all_to_all(share, "ctx", 0, 0, axis_index_groups=same_core, tiled=True)
    shares, anchor = pl.pallas_call(
        project_kernel,
        out_shape=(
            shaped((8, SHARE, 2 * BLK), jnp.bfloat16),
            shaped((2, BLK, HD), jnp.bfloat16),
        ),
        in_specs=[vmem, vmem, vmem],
        out_specs=(vmem, vmem),
        compiler_params=params(),
        cost_estimate=cost(2**28, 0, 2**21),
        name="project",
    )(rows, out_weight, other_weight)
    summands = lax.all_to_all(shares, "tp", 0, 0, tiled=True)
    other_anchor = lax.ppermute(anchor, "ctx", core_swap)
    context_attn = pl.pallas_call(
        block_kernel,
        out_shape=shaped((2 * BLK, HEADS * HD), jnp.bfloat16),
        grid=(2,),
        in_specs=[
            vmem,
            pl.BlockSpec((BLK, HEADS * HD), lambda step: (1 - step, 0)),
            pl.BlockSpec((2, BLK, HD), lambda step: (0, 1 - step, 0)),
            pl.BlockSpec((2, BLK, HD), lambda step: (0, 0, 0)),
            pl.BlockSpec((2, BLK, HD), lambda step: (0, 0, 0)),
            hbm,
        ],
        out_specs=pl.BlockSpec((BLK, HEADS * HD), lambda step: (1 - step, 0)),
        scratch_shapes=[
            pltpu.VMEM((HEADS, BLK, BLK), jnp.float32),
            pltpu.SemaphoreType.DMA,
        ],
        compiler_params=params(),
        cost_estimate=cost(2**30, 2**21, 2**22),
        name="block_attention",
    )(info, ctx_queries, ctx_keyvals, anchor, other_anchor, far(scores))
    summands, context_attn = lax.optimization_barrier((summands, context_attn))
    half_shape = shaped((SHARE, BLK), jnp.float32)
    mine, theirs = pl.pallas_call(
        total_kernel,
        out_shape=(half_shape, half_shape),
        in_specs=[vmem],
        out_specs=(vmem, vmem),
        compiler_params=params(),
        name="plane_sum",
    )(summands)
    theirs = lax.ppermute(theirs, "ctx", core_swap)
    even = lax.axis_index("ctx") % 2 == 0
    window_proj = jnp.concatenate(
        [jnp.where(even, mine, theirs), jnp.where(even, theirs, mine)], axis=0
    )
    return (context_attn, window_proj)


def solution(mesh):
    return jax.shard_map(
        on_device,
        mesh=mesh,
        in_specs=(
            P("ctx", "tp"),
            P(None, "ctx", "tp"),
            P(),
            P(),
            P(None, None, "tp"),
            P(None, None, None, "tp"),
            P("tp", "ctx"),
        ),
        out_specs=(P("ctx", "tp"), P("tp", "ctx")),
        check_vma=False,
    )
```

```python
import math

import jax
import jax.numpy as jnp
from jax import lax
from jax.experimental import pallas as pl
from jax.experimental.pallas import tpu as pltpu
from jax.sharding import PartitionSpec as P

HD = 128
HEADS = 8
BLK = 256
NB = 32
CHIPS = 16
HALF = 128
STAT = 16
PIECE = 32
SHARE = 32
SCALE = 1.0 / math.sqrt(HD)
SCALE2 = SCALE * math.log2(math.e)
AHEAD = 2
masked_score = -1e30

SEND_ROWS = HALF + STAT + PIECE
SHARE_ROWS = HALF + PIECE

same_core = [[chip * 2 + core for chip in range(CHIPS)] for core in range(2)]
same_chip = [
    [(chip * 2 + core) * 8 + plane for core in range(2) for plane in range(8)]
    for chip in range(CHIPS)
]
core_swap = [(device, device ^ 1) for device in range(2 * CHIPS)]

vmem = pl.BlockSpec(memory_space=pltpu.VMEM)
hbm = pl.BlockSpec(memory_space=pltpu.HBM)


def params(room=40):
    return pltpu.CompilerParams(vmem_limit_bytes=room * 2**20)


def cost(flops, exps, size):
    return pl.CostEstimate(flops=flops, transcendentals=exps, bytes_accessed=size)


def split_three(value):
    high = value.astype(jnp.bfloat16)
    rest = value - high.astype(jnp.float32)
    middle = rest.astype(jnp.bfloat16)
    low = (rest - middle.astype(jnp.float32)).astype(jnp.bfloat16)
    return high, middle, low


def dot_nt(left, right):
    return lax.dot_general(
        left, right, (((1,), (1,)), ((), ())), preferred_element_type=jnp.float32
    )


def row_softmax(raw):
    top = jnp.max(raw, axis=1, keepdims=True)
    weights = jnp.exp2((raw - top) * SCALE2)
    return top, jnp.sum(weights, axis=1, keepdims=True), weights


def weigh(weights, values):
    return jnp.dot(weights.astype(jnp.bfloat16), values, preferred_element_type=jnp.float32)


def each_head(query_ref, keys):
    ready = []
    for head in range(HEADS + AHEAD):
        if head < HEADS:
            ready.append(dot_nt(query_ref[:, head * HD : (head + 1) * HD], keys))
        if head >= AHEAD:
            yield head - AHEAD, ready.pop(0)


def read(info_ref, number):
    return jnp.max(info_ref[number : number + 1, :]).astype(jnp.int32)


def own_window(query_ref, window_ref):
    position = lax.axis_index("ctx")
    core = position % 2
    chip = position // 2
    lanes = pl.ds(pl.multiple_of(chip // 2 * HD, HD), HD)
    query = query_ref[chip % 2, :, :, lanes].reshape(HALF, HD)
    raw = dot_nt(query, window_ref[0])
    key = lax.broadcasted_iota(jnp.int32, raw.shape, 1)
    row = lax.broadcasted_iota(jnp.int32, raw.shape, 0)
    row = row // SHARE * (2 * SHARE) + core * SHARE + row % SHARE
    raw = jnp.where(key <= row, raw, masked_score)
    top, total, weights = row_softmax(raw)
    mean = weigh(weights, window_ref[1]) / total
    level = jnp.broadcast_to(top * SCALE + jnp.log(total), (HALF, HALF)).T
    return mean, level[:8]


def fetch_kernel(
    map_hbm,
    reach_hbm,
    query_hbm,
    keyval_hbm,
    window_hbm,
    query_ref,
    keyval_ref,
    window_ref,
    info_ref,
    map_ref,
    reach_ref,
    done,
):
    position = lax.axis_index("ctx")
    core = position % 2
    chip = position // 2
    copies = [
        pltpu.make_async_copy(source, target, done.at[number])
        for number, (source, target) in enumerate(
            (
                (map_hbm, map_ref),
                (reach_hbm, reach_ref),
                (query_hbm.at[:, :, core], query_ref),
                (keyval_hbm, keyval_ref),
                (window_hbm.at[chip % 2], window_ref),
            )
        )
    ]
    for copy in copies:
        copy.start()
    for copy in copies[:2]:
        copy.wait()
    partner = position + 1 - 2 * core

    def put(number, value):
        info_ref[number : number + 1, :] = jnp.full((1, HD), value.astype(jnp.float32))

    holder = jnp.int32(0)
    for number in range(2 * NB):
        holder = jnp.where(map_ref[number] == core * NB, number // 4, holder)
    put(0, holder)
    for part, device in enumerate((position, partner)):
        put(1 + part, map_ref[2 * device] // NB)
        for context in range(2):
            slot = jnp.where(map_ref[2 * device] // NB == context, 0, 1)
            place = map_ref[2 * device + slot] - NB * context
            put(3 + 2 * context + part, jnp.where(place < reach_ref[context], 1, 0))
    slot = jnp.where(map_ref[2 * position] // NB == core, 0, 1)
    put(7, map_ref[2 * position + slot] - NB * core)
    put(8, map_ref[2 * position])
    put(9, map_ref[2 * position + 1])
    for copy in copies[2:]:
        copy.wait()


def window_kernel(
    info_ref,
    query_ref,
    own_ref,
    other_ref,
    window_ref,
    rows_hbm,
    send_ref,
    mean_ref,
    level_ref,
    score_hbm,
    score_ref,
    rows_ref,
    done,
):
    core = lax.axis_index("ctx") % 2
    copy = pltpu.make_async_copy(rows_hbm.at[:BLK], rows_ref, done.at[0])

    @pl.when(core == 0)
    def _():
        copy.start()

    slots = [read(info_ref, 1 + part) for part in range(2)]

    def block_rows(part, context):
        slot = slots[part] if context == 0 else 1 - slots[part]
        return pl.ds(pl.multiple_of(slot * BLK, BLK), BLK)

    sources = (own_ref, other_ref)
    lane = lax.broadcasted_iota(jnp.int32, (BLK, HD), 1)
    columns = jnp.zeros((BLK, HD), jnp.float32)
    steps = [(context, pair) for context in range(2) for pair in range(HEADS // 2)]
    keys = []
    values = []
    biases = []
    for context in range(2):
        rows = [block_rows(part, context) for part in range(2)]
        keys.append(
            jnp.concatenate([ref[0, taken, :] for ref, taken in zip(sources, rows)], axis=0)
        )
        values.append([ref[1, taken, :] for ref, taken in zip(sources, rows)])
        biases.append(
            [
                jnp.where(read(info_ref, number) == 1, 0.0, masked_score)
                for number in (3 + 2 * context, 4 + 2 * context)
            ]
        )

    def score(step):
        context, pair = steps[step]
        query = jnp.concatenate(
            [
                query_ref[context, :, :, head * HD : (head + 1) * HD].reshape(HALF, HD)
                for head in (2 * pair, 2 * pair + 1)
            ],
            axis=0,
        )
        return dot_nt(query, keys[context])

    first = read(info_ref, 7) == 0
    own_rows, other_rows = [
        pl.ds(pl.multiple_of((slots[part] ^ core) * BLK, BLK), BLK) for part in range(2)
    ]
    for member in range(2):
        block = jnp.where(first, own_ref[member, own_rows, :], other_ref[member, other_rows, :])
        send_ref[8 * member : 8 * member + 8, HALF + STAT :, :] = block.reshape(8, PIECE, HD)

    def write_stats(columns, context):
        table = columns.T
        level = table[:HEADS] * SCALE + jnp.log(table[HEADS : 2 * HEADS])
        pieces = [piece.astype(jnp.float32) for piece in split_three(level)]
        row = lax.broadcasted_iota(jnp.int32, (STAT, BLK), 0)
        for pair in range(HEADS // 2):
            stats = jnp.zeros((STAT, BLK), jnp.float32)
            for number, piece in enumerate(pieces):
                stats = jnp.where(row == number, piece[pair : pair + 1], stats)
            stats = stats.astype(jnp.bfloat16)
            for half in range(2):
                target = 2 * (2 * pair + half) + context
                lanes = slice(half * HALF, (half + 1) * HALF)
                send_ref[target, HALF : HALF + STAT, :] = stats[:, lanes]

    ready = [score(step) for step in range(AHEAD)]
    for step, (context, pair) in enumerate(steps):
        if step + AHEAD < len(steps):
            ready.append(score(step + AHEAD))
        raw = ready.pop(0)
        parts = []
        for part in range(2):
            top, total, weights = row_softmax(raw[:, part * BLK : (part + 1) * BLK])
            parts.append(
                (top + biases[context][part], total, weigh(weights, values[context][part]))
            )
        joined = jnp.maximum(parts[0][0], parts[1][0])
        lifts = [jnp.exp2((part[0] - joined) * SCALE2) for part in parts]
        total = parts[0][1] * lifts[0] + parts[1][1] * lifts[1]
        inverse = 1.0 / total
        mean = parts[0][2] * (lifts[0] * inverse) + parts[1][2] * (lifts[1] * inverse)
        mean = mean.astype(jnp.bfloat16)
        for half in range(2):
            target = 2 * (2 * pair + half) + context
            send_ref[target, :HALF, :] = mean[half * HALF : (half + 1) * HALF]
        columns = jnp.where(lane == pair, joined, columns)
        columns = jnp.where(lane == HEADS + pair, total, columns)
        if pair == HEADS // 2 - 1:
            write_stats(columns, context)

    @pl.when(core == 0)
    def _():
        mean_ref[...], level_ref[...] = own_window(query_ref, window_ref)
        copy.wait()
        for head in range(HEADS):
            query = rows_ref[:, head * HD : (head + 1) * HD]
            score_ref[head] = dot_nt(query, own_ref[0, :BLK, :])
        copy_out = pltpu.make_async_copy(score_ref, score_hbm, done.at[1])
        copy_out.start()
        copy_out.wait()


def combine_kernel(
    info_ref, got_ref, mean_in, level_in, query_ref, window_ref, share_ref, mean_ref, level_ref
):
    core = lax.axis_index("ctx") % 2

    @pl.when(core == 0)
    def _():
        mean_ref[...] = mean_in[...]
        level_ref[...] = level_in[...]

    @pl.when(core == 1)
    def _():
        mean_ref[...], level_ref[...] = own_window(query_ref, window_ref)

    levels = []
    for source in range(CHIPS):
        stats = got_ref[source, HALF : HALF + STAT, :].astype(jnp.float32)
        levels.append(stats[0:1] + stats[1:2] + stats[2:3])
    levels.append(level_ref[0:1, :])
    levels = jnp.concatenate(levels, axis=0)
    lifts = jnp.exp(levels - jnp.max(levels, axis=0, keepdims=True))
    lifts = lifts / jnp.sum(lifts, axis=0, keepdims=True)
    count = 3 * (CHIPS + 1)
    source_of = lax.broadcasted_iota(jnp.int32, (count, (CHIPS + 1) * HALF), 0) % (CHIPS + 1)
    column = lax.broadcasted_iota(jnp.int32, (count, (CHIPS + 1) * HALF), 1) // HALF
    spread = jnp.where(source_of == column, 1.0, 0.0).astype(jnp.bfloat16)
    wide = lax.dot_general(
        jnp.concatenate(split_three(lifts), axis=0),
        spread,
        (((0,), (0,)), ((), ())),
        preferred_element_type=jnp.float32,
    )
    joined = mean_ref[...] * wide[:, CHIPS * HALF :]
    for source in range(CHIPS):
        part = got_ref[source, :HALF, :].astype(jnp.float32)
        joined = joined + part * wide[:, source * HALF : (source + 1) * HALF]
    result = joined.astype(jnp.bfloat16)
    piece = got_ref[read(info_ref, 0), HALF + STAT :, :]
    for target in range(CHIPS):
        share_ref[target, :HALF, :] = result
        share_ref[target, HALF:, :] = piece


def project_kernel(rows_ref, own_ref, other_ref, out_ref, anchor_ref):
    rows = jnp.concatenate(
        [
            jnp.concatenate(
                [rows_ref[2 * head + context, :HALF, :] for head in range(HEADS)], axis=1
            )
            for context in range(2)
        ],
        axis=0,
    )
    core = lax.axis_index("ctx") % 2

    def fill(weights):
        for number, ref in enumerate(weights):
            result = jnp.dot(rows, ref[...], preferred_element_type=jnp.float32)
            result = result.reshape(8, SHARE, BLK).astype(out_ref.dtype)
            out_ref[8 * number : 8 * number + 8] = result

    @pl.when(core == 0)
    def _():
        fill((own_ref, other_ref))

    @pl.when(core == 1)
    def _():
        fill((other_ref, own_ref))

    anchor_ref[...] = rows_ref[:, HALF:, :].reshape(2, BLK, HD)


def block_kernel(
    info_ref, query_ref, keyval_ref, own_ref, other_ref, score_hbm, out_ref, score_ref, done
):
    step = pl.program_id(0)
    core = lax.axis_index("ctx") % 2
    scored = (step == 1) & (core == 0)
    block = jnp.where(step == 0, read(info_ref, 9), read(info_ref, 8))
    mine = block // NB == core
    bias = jnp.where(block % NB != 0, 0.0, masked_score)
    copy = pltpu.make_async_copy(score_hbm, score_ref, done)

    @pl.when((step == 0) & (core == 0))
    def _():
        copy.start()


    def anchor(member):
        return jnp.where(mine, own_ref[member], other_ref[member])

    values = jnp.concatenate([anchor(1), keyval_ref[1]], axis=0)
    key = lax.broadcasted_iota(jnp.int32, (BLK, BLK), 1)
    row = lax.broadcasted_iota(jnp.int32, (BLK, BLK), 0)
    live = key <= row

    def finish(head, former, latter):
        raw = jnp.concatenate([former + bias, jnp.where(live, latter, masked_score)], axis=1)
        _, total, weights = row_softmax(raw)
        result = weigh(weights, values) / total
        out_ref[:, head * HD : (head + 1) * HD] = result.astype(jnp.bfloat16)

    @pl.when(scored)
    def _():
        copy.wait()
        for head, raw in each_head(query_ref, anchor(0)):
            finish(head, raw, score_ref[head])

    @pl.when(jnp.logical_not(scored))
    def _():
        keys = jnp.concatenate([anchor(0), keyval_ref[0]], axis=0)
        for head, raw in each_head(query_ref, keys):
            finish(head, raw[:, :BLK], raw[:, BLK:])


def far(array):
    return pltpu.with_memory_space_constraint(array, pltpu.HBM)


def shaped(shape, dtype):
    return jax.ShapeDtypeStruct(shape, dtype)


def on_device(
    ctx_queries, ctx_keyvals, block_map, window_reach, win_queries, win_keyvals, out_weight
):
    other_keyvals = lax.ppermute(ctx_keyvals, "ctx", core_swap)
    halves = win_queries.reshape(2, 4, 2, SHARE, HEADS * HD)
    queries, keyvals, window, info = pl.pallas_call(
        fetch_kernel,
        out_shape=(
            shaped((2, 4, SHARE, HEADS * HD), jnp.bfloat16),
            shaped((2, 2 * BLK, HD), jnp.bfloat16),
            shaped((2, BLK, HD), jnp.bfloat16),
            shaped((16, HD), jnp.float32),
        ),
        in_specs=[hbm] * 5,
        out_specs=(vmem,) * 4,
        scratch_shapes=[
            pltpu.SMEM((2 * NB,), jnp.int32),
            pltpu.SMEM((2,), jnp.int32),
            pltpu.SemaphoreType.DMA((5,)),
        ],
        compiler_params=params(),
        cost_estimate=cost(2**24, 2**15, 2**21),
        name="window_fetch",
    )(
        *(far(array) for array in (block_map, window_reach, halves, ctx_keyvals, win_keyvals))
    )
    queries, other_keyvals, out_weight = lax.optimization_barrier(
        (queries, other_keyvals, out_weight)
    )
    other_weight = lax.ppermute(out_weight, "ctx", core_swap)
    send, own_mean, own_level, scores = pl.pallas_call(
        window_kernel,
        out_shape=(
            shaped((CHIPS, SEND_ROWS, HD), jnp.bfloat16),
            shaped((HALF, HD), jnp.float32),
            shaped((8, HALF), jnp.float32),
            pltpu.HBM((HEADS, BLK, BLK), jnp.float32),
        ),
        in_specs=[vmem] * 5 + [hbm],
        out_specs=(vmem, vmem, vmem, hbm),
        scratch_shapes=[
            pltpu.VMEM((HEADS, BLK, BLK), jnp.float32),
            pltpu.VMEM((BLK, HEADS * HD), jnp.bfloat16),
            pltpu.SemaphoreType.DMA((2,)),
        ],
        compiler_params=params(),
        cost_estimate=cost(2**29, 2**20, 2**21),
        name="window_parts",
    )(info, queries, keyvals, other_keyvals, window, far(ctx_queries))
    send, other_weight = lax.optimization_barrier((send, other_weight))
    got = lax.all_to_all(send, "ctx", 0, 0, axis_index_groups=same_core, tiled=True)
    share = pl.pallas_call(
        combine_kernel,
        out_shape=shaped((CHIPS, SHARE_ROWS, HD), jnp.bfloat16),
        in_specs=[vmem] * 6,
        out_specs=vmem,
        scratch_shapes=[
            pltpu.VMEM((HALF, HD), jnp.float32),
            pltpu.VMEM((8, HALF), jnp.float32),
        ],
        compiler_params=params(),
        cost_estimate=cost(2**20, 2**12, 2**20),
        name="window_join",
    )(info, got, own_mean, own_level, queries, window)
    rows = lax.all_to_all(share, "ctx", 0, 0, axis_index_groups=same_core, tiled=True)
    shares, anchor = pl.pallas_call(
        project_kernel,
        out_shape=(
            shaped((2 * 8, SHARE, BLK), jnp.bfloat16),
            shaped((2, BLK, HD), jnp.bfloat16),
        ),
        in_specs=[vmem, vmem, vmem],
        out_specs=(vmem, vmem),
        compiler_params=params(),
        cost_estimate=cost(2**28, 0, 2**21),
        name="project",
    )(rows, out_weight, other_weight)
    summands = lax.all_to_all(
        shares, ("ctx", "tp"), 0, 0, axis_index_groups=same_chip, tiled=True
    )
    other_anchor = lax.ppermute(anchor, "ctx", core_swap)
    context_attn = pl.pallas_call(
        block_kernel,
        out_shape=shaped((2 * BLK, HEADS * HD), jnp.bfloat16),
        grid=(2,),
        in_specs=[
            vmem,
            pl.BlockSpec((BLK, HEADS * HD), lambda step: (1 - step, 0)),
            pl.BlockSpec((2, BLK, HD), lambda step: (0, 1 - step, 0)),
            pl.BlockSpec((2, BLK, HD), lambda step: (0, 0, 0)),
            pl.BlockSpec((2, BLK, HD), lambda step: (0, 0, 0)),
            hbm,
        ],
        out_specs=pl.BlockSpec((BLK, HEADS * HD), lambda step: (1 - step, 0)),
        scratch_shapes=[
            pltpu.VMEM((HEADS, BLK, BLK), jnp.float32),
            pltpu.SemaphoreType.DMA,
        ],
        compiler_params=params(),
        cost_estimate=cost(2**30, 2**21, 2**22),
        name="block_attention",
    )(info, ctx_queries, ctx_keyvals, anchor, other_anchor, far(scores))
    summands, context_attn = lax.optimization_barrier((summands, context_attn))
    summands = summands.reshape(2, 8, SHARE, BLK).astype(jnp.float32)
    window_proj = jnp.sum(summands, axis=1).reshape(2 * SHARE, BLK)
    return (context_attn, window_proj)


def solution(mesh):
    return jax.shard_map(
        on_device,
        mesh=mesh,
        in_specs=(
            P("ctx", "tp"),
            P(None, "ctx", "tp"),
            P(),
            P(),
            P(None, None, "tp"),
            P(None, None, None, "tp"),
            P("tp", "ctx"),
        ),
        out_specs=(P("ctx", "tp"), P("tp", "ctx")),
        check_vma=False,
    )
```

```python
import math

import jax
import jax.numpy as jnp
from jax import lax
from jax.experimental import pallas as pl
from jax.experimental.pallas import tpu as pltpu
from jax.sharding import PartitionSpec as P

HD = 128
HEADS = 8
BLK = 256
NB = 32
CHIPS = 16
HALF = 128
STAT = 16
PIECE = 32
SHARE = 32
SCALE = 1.0 / math.sqrt(HD)
SCALE2 = SCALE * math.log2(math.e)
AHEAD = 2
EARLY = 4
masked_score = -1e30

SEND_ROWS = HALF + STAT + PIECE
SHARE_ROWS = HALF + PIECE

same_core = [[chip * 2 + core for chip in range(CHIPS)] for core in range(2)]
same_chip = [
    [(chip * 2 + core) * 8 + plane for core in range(2) for plane in range(8)]
    for chip in range(CHIPS)
]
core_swap = [(device, device ^ 1) for device in range(2 * CHIPS)]

vmem = pl.BlockSpec(memory_space=pltpu.VMEM)
hbm = pl.BlockSpec(memory_space=pltpu.HBM)


def params(room=40):
    return pltpu.CompilerParams(vmem_limit_bytes=room * 2**20)


def cost(flops, exps, size):
    return pl.CostEstimate(flops=flops, transcendentals=exps, bytes_accessed=size)


def split_three(value):
    high = value.astype(jnp.bfloat16)
    rest = value - high.astype(jnp.float32)
    middle = rest.astype(jnp.bfloat16)
    low = (rest - middle.astype(jnp.float32)).astype(jnp.bfloat16)
    return high, middle, low


def dot_nt(left, right):
    return lax.dot_general(
        left, right, (((1,), (1,)), ((), ())), preferred_element_type=jnp.float32
    )


def row_softmax(raw):
    top = jnp.max(raw, axis=1, keepdims=True)
    weights = jnp.exp2((raw - top) * SCALE2)
    return top, jnp.sum(weights, axis=1, keepdims=True), weights


def weigh(weights, values):
    return jnp.dot(weights.astype(jnp.bfloat16), values, preferred_element_type=jnp.float32)


def each_head(query_ref, keys):
    ready = []
    for head in range(HEADS + AHEAD):
        if head < HEADS:
            ready.append(dot_nt(query_ref[:, head * HD : (head + 1) * HD], keys))
        if head >= AHEAD:
            yield head - AHEAD, ready.pop(0)


def staged(score, count):
    ready = []
    for step in range(count + AHEAD):
        if step < count:
            ready.append(score(step))
        if step >= AHEAD:
            yield step - AHEAD, ready.pop(0)


steps = [(context, pair) for context in range(2) for pair in range(HEADS // 2)]


def pair_query(query_ref, step):
    context, pair = steps[step]
    return jnp.concatenate(
        [
            query_ref[context, :, :, head * HD : (head + 1) * HD].reshape(HALF, HD)
            for head in (2 * pair, 2 * pair + 1)
        ],
        axis=0,
    )


def read(info_ref, number):
    return jnp.max(info_ref[number : number + 1, :]).astype(jnp.int32)


def own_window(query_ref, window_ref):
    position = lax.axis_index("ctx")
    core = position % 2
    chip = position // 2
    lanes = pl.ds(pl.multiple_of(chip // 2 * HD, HD), HD)
    query = query_ref[chip % 2, :, :, lanes].reshape(HALF, HD)
    raw = dot_nt(query, window_ref[0])
    key = lax.broadcasted_iota(jnp.int32, raw.shape, 1)
    row = lax.broadcasted_iota(jnp.int32, raw.shape, 0)
    row = row // SHARE * (2 * SHARE) + core * SHARE + row % SHARE
    raw = jnp.where(key <= row, raw, masked_score)
    top, total, weights = row_softmax(raw)
    mean = weigh(weights, window_ref[1]) / total
    level = jnp.broadcast_to(top * SCALE + jnp.log(total), (HALF, HALF)).T
    return mean, level[:8]


def fetch_kernel(
    map_hbm,
    reach_hbm,
    query_hbm,
    keyval_hbm,
    window_hbm,
    query_ref,
    keyval_ref,
    window_ref,
    info_ref,
    table_ref,
    map_ref,
    reach_ref,
    done,
):
    position = lax.axis_index("ctx")
    core = position % 2
    chip = position // 2
    copies = [
        pltpu.make_async_copy(source, target, done.at[number])
        for number, (source, target) in enumerate(
            (
                (map_hbm, map_ref),
                (reach_hbm, reach_ref),
                (query_hbm.at[:, :, core], query_ref),
                (keyval_hbm, keyval_ref),
                (window_hbm.at[chip % 2], window_ref),
            )
        )
    ]
    for copy in copies:
        copy.start()
    for copy in copies[:2]:
        copy.wait()
    partner = position + 1 - 2 * core

    def put(number, value):
        info_ref[number : number + 1, :] = jnp.full((1, HD), value.astype(jnp.float32))

    holder = jnp.int32(0)
    for number in range(2 * NB):
        holder = jnp.where(map_ref[number] == core * NB, number // 4, holder)
    put(0, holder)
    for part, device in enumerate((position, partner)):
        put(1 + part, map_ref[2 * device] // NB)
        for context in range(2):
            slot = jnp.where(map_ref[2 * device] // NB == context, 0, 1)
            place = map_ref[2 * device + slot] - NB * context
            put(3 + 2 * context + part, jnp.where(place < reach_ref[context], 1, 0))
    slot = jnp.where(map_ref[2 * position] // NB == core, 0, 1)
    put(7, map_ref[2 * position + slot] - NB * core)
    put(8, map_ref[2 * position])
    put(9, map_ref[2 * position + 1])
    for copy in copies[2:]:
        copy.wait()

    @pl.when(core == 1)
    def _():
        taken = pl.ds(pl.multiple_of(map_ref[2 * position] // NB * BLK, BLK), BLK)
        keys, values = keyval_ref[0, taken, :], keyval_ref[1, taken, :]
        for step, raw in staged(lambda step: dot_nt(pair_query(query_ref, step), keys), EARLY):
            top, total, weights = row_softmax(raw)
            table_ref[0, step] = jnp.broadcast_to(top, (BLK, HD))
            table_ref[1, step] = jnp.broadcast_to(total, (BLK, HD))
            table_ref[2, step] = weigh(weights, values)


def window_kernel(
    info_ref,
    query_ref,
    own_ref,
    other_ref,
    window_ref,
    table_ref,
    rows_hbm,
    send_ref,
    mean_ref,
    level_ref,
    score_hbm,
    score_ref,
    rows_ref,
    done,
):
    core = lax.axis_index("ctx") % 2
    copy = pltpu.make_async_copy(rows_hbm.at[:BLK], rows_ref, done.at[0])

    @pl.when(core == 0)
    def _():
        copy.start()

    slots = [read(info_ref, 1 + part) for part in range(2)]

    def block_rows(part, context):
        slot = slots[part] if context == 0 else 1 - slots[part]
        return pl.ds(pl.multiple_of(slot * BLK, BLK), BLK)

    sources = (own_ref, other_ref)
    lane = lax.broadcasted_iota(jnp.int32, (BLK, HD), 1)
    keys = []
    values = []
    biases = []
    for context in range(2):
        rows = [block_rows(part, context) for part in range(2)]
        keys.append([ref[0, taken, :] for ref, taken in zip(sources, rows)])
        values.append([ref[1, taken, :] for ref, taken in zip(sources, rows)])
        biases.append(
            [
                jnp.where(read(info_ref, number) == 1, 0.0, masked_score)
                for number in (3 + 2 * context, 4 + 2 * context)
            ]
        )

    first = read(info_ref, 7) == 0
    own_rows, other_rows = [
        pl.ds(pl.multiple_of((slots[part] ^ core) * BLK, BLK), BLK) for part in range(2)
    ]
    for member in range(2):
        block = jnp.where(first, own_ref[member, own_rows, :], other_ref[member, other_rows, :])
        send_ref[8 * member : 8 * member + 8, HALF + STAT :, :] = block.reshape(8, PIECE, HD)

    def write_stats(columns, context):
        table = columns.T
        level = table[:HEADS] * SCALE + jnp.log(table[HEADS : 2 * HEADS])
        pieces = [piece.astype(jnp.float32) for piece in split_three(level)]
        row = lax.broadcasted_iota(jnp.int32, (STAT, BLK), 0)
        for pair in range(HEADS // 2):
            stats = jnp.zeros((STAT, BLK), jnp.float32)
            for number, piece in enumerate(pieces):
                stats = jnp.where(row == number, piece[pair : pair + 1], stats)
            stats = stats.astype(jnp.bfloat16)
            for half in range(2):
                target = 2 * (2 * pair + half) + context
                lanes = slice(half * HALF, (half + 1) * HALF)
                send_ref[target, HALF : HALF + STAT, :] = stats[:, lanes]

    def part_of(raw, step, part):
        top, total, weights = row_softmax(raw)
        return top, total, weigh(weights, values[steps[step][0]][part])

    def merge(step, parts, columns):
        context, pair = steps[step]
        tops = [part[0] + bias for part, bias in zip(parts, biases[context])]
        joined = jnp.maximum(tops[0], tops[1])
        lifts = [jnp.exp2((top - joined) * SCALE2) for top in tops]
        total = parts[0][1] * lifts[0] + parts[1][1] * lifts[1]
        inverse = 1.0 / total
        mean = parts[0][2] * (lifts[0] * inverse) + parts[1][2] * (lifts[1] * inverse)
        mean = mean.astype(jnp.bfloat16)
        for half in range(2):
            target = 2 * (2 * pair + half) + context
            send_ref[target, :HALF, :] = mean[half * HALF : (half + 1) * HALF]
        if pair == 0:
            columns = jnp.zeros((BLK, HD), jnp.float32)
        columns = jnp.where(lane == pair, joined, columns)
        columns = jnp.where(lane == HEADS + pair, total, columns)
        if pair == HEADS // 2 - 1:
            write_stats(columns, context)
        return columns

    both = [jnp.concatenate(pair, axis=0) for pair in keys]

    def run(early):
        columns = None

        def score(step):
            context = steps[step][0]
            return dot_nt(
                pair_query(query_ref, step), keys[context][1] if step < early else both[context]
            )

        for step, raw in staged(score, len(steps)):
            if step < early:
                parts = [[table_ref[number, step] for number in range(3)], part_of(raw, step, 1)]
            else:
                parts = [
                    part_of(raw[:, part * BLK : (part + 1) * BLK], step, part)
                    for part in range(2)
                ]
            columns = merge(step, parts, columns)

    @pl.when(core == 0)
    def _():
        run(0)

    @pl.when(core == 1)
    def _():
        run(EARLY)

    @pl.when(core == 0)
    def _():
        mean_ref[...], level_ref[...] = own_window(query_ref, window_ref)
        copy.wait()
        for head in range(HEADS):
            query = rows_ref[:, head * HD : (head + 1) * HD]
            score_ref[head] = dot_nt(query, own_ref[0, :BLK, :])
        copy_out = pltpu.make_async_copy(score_ref, score_hbm, done.at[1])
        copy_out.start()
        copy_out.wait()


def combine_kernel(
    info_ref, got_ref, mean_in, level_in, query_ref, window_ref, share_ref, mean_ref, level_ref
):
    core = lax.axis_index("ctx") % 2

    @pl.when(core == 0)
    def _():
        mean_ref[...] = mean_in[...]
        level_ref[...] = level_in[...]

    @pl.when(core == 1)
    def _():
        mean_ref[...], level_ref[...] = own_window(query_ref, window_ref)

    levels = []
    for source in range(CHIPS):
        stats = got_ref[source, HALF : HALF + STAT, :].astype(jnp.float32)
        levels.append(stats[0:1] + stats[1:2] + stats[2:3])
    levels.append(level_ref[0:1, :])
    levels = jnp.concatenate(levels, axis=0)
    lifts = jnp.exp(levels - jnp.max(levels, axis=0, keepdims=True))
    lifts = lifts / jnp.sum(lifts, axis=0, keepdims=True)
    count = 3 * (CHIPS + 1)
    source_of = lax.broadcasted_iota(jnp.int32, (count, (CHIPS + 1) * HALF), 0) % (CHIPS + 1)
    column = lax.broadcasted_iota(jnp.int32, (count, (CHIPS + 1) * HALF), 1) // HALF
    spread = jnp.where(source_of == column, 1.0, 0.0).astype(jnp.bfloat16)
    wide = lax.dot_general(
        jnp.concatenate(split_three(lifts), axis=0),
        spread,
        (((0,), (0,)), ((), ())),
        preferred_element_type=jnp.float32,
    )
    joined = mean_ref[...] * wide[:, CHIPS * HALF :]
    for source in range(CHIPS):
        part = got_ref[source, :HALF, :].astype(jnp.float32)
        joined = joined + part * wide[:, source * HALF : (source + 1) * HALF]
    result = joined.astype(jnp.bfloat16)
    piece = got_ref[read(info_ref, 0), HALF + STAT :, :]
    for target in range(CHIPS):
        share_ref[target, :HALF, :] = result
        share_ref[target, HALF:, :] = piece


def project_kernel(rows_ref, own_ref, other_ref, out_ref, anchor_ref):
    rows = jnp.concatenate(
        [
            jnp.concatenate(
                [rows_ref[2 * head + context, :HALF, :] for head in range(HEADS)], axis=1
            )
            for context in range(2)
        ],
        axis=0,
    )
    core = lax.axis_index("ctx") % 2

    def fill(weights):
        for number, ref in enumerate(weights):
            result = jnp.dot(rows, ref[...], preferred_element_type=jnp.float32)
            result = result.reshape(8, SHARE, BLK).astype(out_ref.dtype)
            out_ref[8 * number : 8 * number + 8] = result

    @pl.when(core == 0)
    def _():
        fill((own_ref, other_ref))

    @pl.when(core == 1)
    def _():
        fill((other_ref, own_ref))

    anchor_ref[...] = rows_ref[:, HALF:, :].reshape(2, BLK, HD)


def block_kernel(
    info_ref, query_ref, keyval_ref, own_ref, other_ref, score_hbm, out_ref, score_ref, done
):
    step = pl.program_id(0)
    core = lax.axis_index("ctx") % 2
    scored = (step == 1) & (core == 0)
    block = jnp.where(step == 0, read(info_ref, 9), read(info_ref, 8))
    mine = block // NB == core
    bias = jnp.where(block % NB != 0, 0.0, masked_score)
    copy = pltpu.make_async_copy(score_hbm, score_ref, done)

    @pl.when((step == 0) & (core == 0))
    def _():
        copy.start()


    def anchor(member):
        return jnp.where(mine, own_ref[member], other_ref[member])

    values = jnp.concatenate([anchor(1), keyval_ref[1]], axis=0)
    key = lax.broadcasted_iota(jnp.int32, (BLK, BLK), 1)
    row = lax.broadcasted_iota(jnp.int32, (BLK, BLK), 0)
    live = key <= row

    def finish(head, former, latter):
        raw = jnp.concatenate([former + bias, jnp.where(live, latter, masked_score)], axis=1)
        _, total, weights = row_softmax(raw)
        result = weigh(weights, values) / total
        out_ref[:, head * HD : (head + 1) * HD] = result.astype(jnp.bfloat16)

    @pl.when(scored)
    def _():
        copy.wait()
        for head, raw in each_head(query_ref, anchor(0)):
            finish(head, raw, score_ref[head])

    @pl.when(jnp.logical_not(scored))
    def _():
        keys = jnp.concatenate([anchor(0), keyval_ref[0]], axis=0)
        for head, raw in each_head(query_ref, keys):
            finish(head, raw[:, :BLK], raw[:, BLK:])


def far(array):
    return pltpu.with_memory_space_constraint(array, pltpu.HBM)


def shaped(shape, dtype):
    return jax.ShapeDtypeStruct(shape, dtype)


def on_device(
    ctx_queries, ctx_keyvals, block_map, window_reach, win_queries, win_keyvals, out_weight
):
    other_keyvals = lax.ppermute(ctx_keyvals, "ctx", core_swap)
    halves = win_queries.reshape(2, 4, 2, SHARE, HEADS * HD)
    queries, keyvals, window, info, table = pl.pallas_call(
        fetch_kernel,
        out_shape=(
            shaped((2, 4, SHARE, HEADS * HD), jnp.bfloat16),
            shaped((2, 2 * BLK, HD), jnp.bfloat16),
            shaped((2, BLK, HD), jnp.bfloat16),
            shaped((16, HD), jnp.float32),
            shaped((3, EARLY, BLK, HD), jnp.float32),
        ),
        in_specs=[hbm] * 5,
        out_specs=(vmem,) * 5,
        scratch_shapes=[
            pltpu.SMEM((2 * NB,), jnp.int32),
            pltpu.SMEM((2,), jnp.int32),
            pltpu.SemaphoreType.DMA((5,)),
        ],
        compiler_params=params(),
        cost_estimate=cost(2**24, 2**15, 2**21),
        name="window_fetch",
    )(
        *(far(array) for array in (block_map, window_reach, halves, ctx_keyvals, win_keyvals))
    )
    queries, other_keyvals, out_weight = lax.optimization_barrier(
        (queries, other_keyvals, out_weight)
    )
    other_weight = lax.ppermute(out_weight, "ctx", core_swap)
    send, own_mean, own_level, scores = pl.pallas_call(
        window_kernel,
        out_shape=(
            shaped((CHIPS, SEND_ROWS, HD), jnp.bfloat16),
            shaped((HALF, HD), jnp.float32),
            shaped((8, HALF), jnp.float32),
            pltpu.HBM((HEADS, BLK, BLK), jnp.float32),
        ),
        in_specs=[vmem] * 6 + [hbm],
        out_specs=(vmem, vmem, vmem, hbm),
        scratch_shapes=[
            pltpu.VMEM((HEADS, BLK, BLK), jnp.float32),
            pltpu.VMEM((BLK, HEADS * HD), jnp.bfloat16),
            pltpu.SemaphoreType.DMA((2,)),
        ],
        compiler_params=params(),
        cost_estimate=cost(2**29, 2**20, 2**21),
        name="window_parts",
    )(info, queries, keyvals, other_keyvals, window, table, far(ctx_queries))
    send, other_weight = lax.optimization_barrier((send, other_weight))
    got = lax.all_to_all(send, "ctx", 0, 0, axis_index_groups=same_core, tiled=True)
    share = pl.pallas_call(
        combine_kernel,
        out_shape=shaped((CHIPS, SHARE_ROWS, HD), jnp.bfloat16),
        in_specs=[vmem] * 6,
        out_specs=vmem,
        scratch_shapes=[
            pltpu.VMEM((HALF, HD), jnp.float32),
            pltpu.VMEM((8, HALF), jnp.float32),
        ],
        compiler_params=params(),
        cost_estimate=cost(2**20, 2**12, 2**20),
        name="window_join",
    )(info, got, own_mean, own_level, queries, window)
    rows = lax.all_to_all(share, "ctx", 0, 0, axis_index_groups=same_core, tiled=True)
    shares, anchor = pl.pallas_call(
        project_kernel,
        out_shape=(
            shaped((2 * 8, SHARE, BLK), jnp.bfloat16),
            shaped((2, BLK, HD), jnp.bfloat16),
        ),
        in_specs=[vmem, vmem, vmem],
        out_specs=(vmem, vmem),
        compiler_params=params(),
        cost_estimate=cost(2**28, 0, 2**21),
        name="project",
    )(rows, out_weight, other_weight)
    summands = lax.all_to_all(
        shares, ("ctx", "tp"), 0, 0, axis_index_groups=same_chip, tiled=True
    )
    other_anchor = lax.ppermute(anchor, "ctx", core_swap)
    context_attn = pl.pallas_call(
        block_kernel,
        out_shape=shaped((2 * BLK, HEADS * HD), jnp.bfloat16),
        grid=(2,),
        in_specs=[
            vmem,
            pl.BlockSpec((BLK, HEADS * HD), lambda step: (1 - step, 0)),
            pl.BlockSpec((2, BLK, HD), lambda step: (0, 1 - step, 0)),
            pl.BlockSpec((2, BLK, HD), lambda step: (0, 0, 0)),
            pl.BlockSpec((2, BLK, HD), lambda step: (0, 0, 0)),
            hbm,
        ],
        out_specs=pl.BlockSpec((BLK, HEADS * HD), lambda step: (1 - step, 0)),
        scratch_shapes=[
            pltpu.VMEM((HEADS, BLK, BLK), jnp.float32),
            pltpu.SemaphoreType.DMA,
        ],
        compiler_params=params(),
        cost_estimate=cost(2**30, 2**21, 2**22),
        name="block_attention",
    )(info, ctx_queries, ctx_keyvals, anchor, other_anchor, far(scores))
    summands, context_attn = lax.optimization_barrier((summands, context_attn))
    summands = summands.reshape(2, 8, SHARE, BLK).astype(jnp.float32)
    window_proj = jnp.sum(summands, axis=1).reshape(2 * SHARE, BLK)
    return (context_attn, window_proj)


def solution(mesh):
    return jax.shard_map(
        on_device,
        mesh=mesh,
        in_specs=(
            P("ctx", "tp"),
            P(None, "ctx", "tp"),
            P(),
            P(),
            P(None, None, "tp"),
            P(None, None, None, "tp"),
            P("tp", "ctx"),
        ),
        out_specs=(P("ctx", "tp"), P("tp", "ctx")),
        check_vma=False,
    )
```

```python
import math

import jax
import jax.numpy as jnp
from jax import lax
from jax.experimental import pallas as pl
from jax.experimental.pallas import tpu as pltpu
from jax.sharding import PartitionSpec as P

HD = 128
HEADS = 8
BLK = 256
NB = 32
CHIPS = 16
HALF = 128
STAT = 16
PIECE = 32
SHARE = 32
SCALE = 1.0 / math.sqrt(HD)
SCALE2 = SCALE * math.log2(math.e)
AHEAD = 2
masked_score = -1e30

SEND_ROWS = HALF + STAT + PIECE
SHARE_ROWS = HALF + PIECE

same_core = [
    [(place + core * CHIPS // 2) % CHIPS * 2 + core for place in range(CHIPS)]
    for core in range(2)
]
same_chip = [
    [(chip * 2 + core) * 8 + plane for core in range(2) for plane in range(8)]
    for chip in range(CHIPS)
]
core_swap = [(device, device ^ 1) for device in range(2 * CHIPS)]

vmem = pl.BlockSpec(memory_space=pltpu.VMEM)
hbm = pl.BlockSpec(memory_space=pltpu.HBM)


def params(room=40):
    return pltpu.CompilerParams(vmem_limit_bytes=room * 2**20)


def cost(flops, exps, size):
    return pl.CostEstimate(flops=flops, transcendentals=exps, bytes_accessed=size)


def split_three(value):
    high = value.astype(jnp.bfloat16)
    rest = value - high.astype(jnp.float32)
    middle = rest.astype(jnp.bfloat16)
    low = (rest - middle.astype(jnp.float32)).astype(jnp.bfloat16)
    return high, middle, low


def dot_nt(left, right):
    return lax.dot_general(
        left, right, (((1,), (1,)), ((), ())), preferred_element_type=jnp.float32
    )


def row_softmax(raw):
    top = jnp.max(raw, axis=1, keepdims=True)
    weights = jnp.exp2((raw - top) * SCALE2)
    return top, jnp.sum(weights, axis=1, keepdims=True), weights


def weigh(weights, values):
    return jnp.dot(weights.astype(jnp.bfloat16), values, preferred_element_type=jnp.float32)


def each_head(query_ref, keys):
    ready = []
    for head in range(HEADS + AHEAD):
        if head < HEADS:
            ready.append(dot_nt(query_ref[:, head * HD : (head + 1) * HD], keys))
        if head >= AHEAD:
            yield head - AHEAD, ready.pop(0)


def read(info_ref, number):
    return jnp.max(info_ref[number : number + 1, :]).astype(jnp.int32)


def own_window(query_ref, window_ref):
    position = lax.axis_index("ctx")
    core = position % 2
    chip = (position // 2 + core * (CHIPS // 2)) % CHIPS
    lanes = pl.ds(pl.multiple_of(chip // 2 * HD, HD), HD)
    query = query_ref[chip % 2, :, :, lanes].reshape(HALF, HD)
    raw = dot_nt(query, window_ref[0])
    key = lax.broadcasted_iota(jnp.int32, raw.shape, 1)
    row = lax.broadcasted_iota(jnp.int32, raw.shape, 0)
    row = row // SHARE * (2 * SHARE) + core * SHARE + row % SHARE
    raw = jnp.where(key <= row, raw, masked_score)
    top, total, weights = row_softmax(raw)
    mean = weigh(weights, window_ref[1]) / total
    level = jnp.broadcast_to(top * SCALE + jnp.log(total), (HALF, HALF)).T
    return mean, level[:8]


def fetch_kernel(
    map_hbm,
    reach_hbm,
    query_hbm,
    keyval_hbm,
    window_hbm,
    query_ref,
    keyval_ref,
    window_ref,
    info_ref,
    map_ref,
    reach_ref,
    done,
):
    position = lax.axis_index("ctx")
    core = position % 2
    chip = (position // 2 + core * (CHIPS // 2)) % CHIPS
    copies = [
        pltpu.make_async_copy(source, target, done.at[number])
        for number, (source, target) in enumerate(
            (
                (map_hbm, map_ref),
                (reach_hbm, reach_ref),
                (query_hbm.at[:, :, core], query_ref),
                (keyval_hbm, keyval_ref),
                (window_hbm.at[chip % 2], window_ref),
            )
        )
    ]
    for copy in copies:
        copy.start()
    for copy in copies[:2]:
        copy.wait()
    partner = position + 1 - 2 * core

    def put(number, value):
        info_ref[number : number + 1, :] = jnp.full((1, HD), value.astype(jnp.float32))

    holder = jnp.int32(0)
    for number in range(2 * NB):
        holder = jnp.where(map_ref[number] == core * NB, number // 4, holder)
    put(0, (holder + core * (CHIPS // 2)) % CHIPS)
    for part, device in enumerate((position, partner)):
        put(1 + part, map_ref[2 * device] // NB)
        for context in range(2):
            slot = jnp.where(map_ref[2 * device] // NB == context, 0, 1)
            place = map_ref[2 * device + slot] - NB * context
            put(3 + 2 * context + part, jnp.where(place < reach_ref[context], 1, 0))
    slot = jnp.where(map_ref[2 * position] // NB == core, 0, 1)
    put(7, map_ref[2 * position + slot] - NB * core)
    put(8, map_ref[2 * position])
    put(9, map_ref[2 * position + 1])
    for copy in copies[2:]:
        copy.wait()


def window_kernel(
    info_ref,
    query_ref,
    own_ref,
    other_ref,
    window_ref,
    rows_hbm,
    send_ref,
    mean_ref,
    level_ref,
    score_hbm,
    score_ref,
    rows_ref,
    done,
):
    core = lax.axis_index("ctx") % 2
    copy = pltpu.make_async_copy(rows_hbm.at[:BLK], rows_ref, done.at[0])

    @pl.when(core == 0)
    def _():
        copy.start()

    slots = [read(info_ref, 1 + part) for part in range(2)]

    def block_rows(part, context):
        slot = slots[part] if context == 0 else 1 - slots[part]
        return pl.ds(pl.multiple_of(slot * BLK, BLK), BLK)

    sources = (own_ref, other_ref)
    lane = lax.broadcasted_iota(jnp.int32, (BLK, HD), 1)
    columns = jnp.zeros((BLK, HD), jnp.float32)
    steps = [(context, pair) for context in range(2) for pair in range(HEADS // 2)]
    keys = []
    values = []
    biases = []
    for context in range(2):
        rows = [block_rows(part, context) for part in range(2)]
        keys.append(
            jnp.concatenate([ref[0, taken, :] for ref, taken in zip(sources, rows)], axis=0)
        )
        values.append([ref[1, taken, :] for ref, taken in zip(sources, rows)])
        biases.append(
            [
                jnp.where(read(info_ref, number) == 1, 0.0, masked_score)
                for number in (3 + 2 * context, 4 + 2 * context)
            ]
        )

    def score(step):
        context, pair = steps[step]
        query = jnp.concatenate(
            [
                query_ref[context, :, :, head * HD : (head + 1) * HD].reshape(HALF, HD)
                for head in (2 * pair, 2 * pair + 1)
            ],
            axis=0,
        )
        return dot_nt(query, keys[context])

    first = read(info_ref, 7) == 0
    own_rows, other_rows = [
        pl.ds(pl.multiple_of((slots[part] ^ core) * BLK, BLK), BLK) for part in range(2)
    ]
    for member in range(2):
        block = jnp.where(first, own_ref[member, own_rows, :], other_ref[member, other_rows, :])
        send_ref[8 * member : 8 * member + 8, HALF + STAT :, :] = block.reshape(8, PIECE, HD)

    def write_stats(columns, context):
        table = columns.T
        level = table[:HEADS] * SCALE + jnp.log(table[HEADS : 2 * HEADS])
        pieces = [piece.astype(jnp.float32) for piece in split_three(level)]
        row = lax.broadcasted_iota(jnp.int32, (STAT, BLK), 0)
        for pair in range(HEADS // 2):
            stats = jnp.zeros((STAT, BLK), jnp.float32)
            for number, piece in enumerate(pieces):
                stats = jnp.where(row == number, piece[pair : pair + 1], stats)
            stats = stats.astype(jnp.bfloat16)
            for half in range(2):
                target = 2 * (2 * pair + half) + context
                lanes = slice(half * HALF, (half + 1) * HALF)
                send_ref[target, HALF : HALF + STAT, :] = stats[:, lanes]

    ready = [score(step) for step in range(AHEAD)]
    for step, (context, pair) in enumerate(steps):
        if step + AHEAD < len(steps):
            ready.append(score(step + AHEAD))
        raw = ready.pop(0)
        parts = []
        for part in range(2):
            top, total, weights = row_softmax(raw[:, part * BLK : (part + 1) * BLK])
            parts.append(
                (top + biases[context][part], total, weigh(weights, values[context][part]))
            )
        joined = jnp.maximum(parts[0][0], parts[1][0])
        lifts = [jnp.exp2((part[0] - joined) * SCALE2) for part in parts]
        total = parts[0][1] * lifts[0] + parts[1][1] * lifts[1]
        inverse = 1.0 / total
        mean = parts[0][2] * (lifts[0] * inverse) + parts[1][2] * (lifts[1] * inverse)
        mean = mean.astype(jnp.bfloat16)
        for half in range(2):
            target = 2 * (2 * pair + half) + context
            send_ref[target, :HALF, :] = mean[half * HALF : (half + 1) * HALF]
        columns = jnp.where(lane == pair, joined, columns)
        columns = jnp.where(lane == HEADS + pair, total, columns)
        if pair == HEADS // 2 - 1:
            write_stats(columns, context)

    @pl.when(core == 0)
    def _():
        mean_ref[...], level_ref[...] = own_window(query_ref, window_ref)
        copy.wait()
        for head in range(HEADS):
            query = rows_ref[:, head * HD : (head + 1) * HD]
            score_ref[head] = dot_nt(query, own_ref[0, :BLK, :])
        copy_out = pltpu.make_async_copy(score_ref, score_hbm, done.at[1])
        copy_out.start()
        copy_out.wait()


def combine_kernel(
    info_ref, got_ref, mean_in, level_in, query_ref, window_ref, share_ref, mean_ref, level_ref
):
    core = lax.axis_index("ctx") % 2

    @pl.when(core == 0)
    def _():
        mean_ref[...] = mean_in[...]
        level_ref[...] = level_in[...]

    @pl.when(core == 1)
    def _():
        mean_ref[...], level_ref[...] = own_window(query_ref, window_ref)

    levels = []
    for source in range(CHIPS):
        stats = got_ref[source, HALF : HALF + STAT, :].astype(jnp.float32)
        levels.append(stats[0:1] + stats[1:2] + stats[2:3])
    levels.append(level_ref[0:1, :])
    levels = jnp.concatenate(levels, axis=0)
    lifts = jnp.exp(levels - jnp.max(levels, axis=0, keepdims=True))
    lifts = lifts / jnp.sum(lifts, axis=0, keepdims=True)
    count = 3 * (CHIPS + 1)
    source_of = lax.broadcasted_iota(jnp.int32, (count, (CHIPS + 1) * HALF), 0) % (CHIPS + 1)
    column = lax.broadcasted_iota(jnp.int32, (count, (CHIPS + 1) * HALF), 1) // HALF
    spread = jnp.where(source_of == column, 1.0, 0.0).astype(jnp.bfloat16)
    wide = lax.dot_general(
        jnp.concatenate(split_three(lifts), axis=0),
        spread,
        (((0,), (0,)), ((), ())),
        preferred_element_type=jnp.float32,
    )
    joined = mean_ref[...] * wide[:, CHIPS * HALF :]
    for source in range(CHIPS):
        part = got_ref[source, :HALF, :].astype(jnp.float32)
        joined = joined + part * wide[:, source * HALF : (source + 1) * HALF]
    result = joined.astype(jnp.bfloat16)
    piece = got_ref[read(info_ref, 0), HALF + STAT :, :]
    for target in range(CHIPS):
        share_ref[target, :HALF, :] = result
        share_ref[target, HALF:, :] = piece


def project_kernel(rows_ref, own_ref, other_ref, out_ref, anchor_ref):
    rows = jnp.concatenate(
        [
            jnp.concatenate(
                [rows_ref[2 * head + context, :HALF, :] for head in range(HEADS)], axis=1
            )
            for context in range(2)
        ],
        axis=0,
    )
    core = lax.axis_index("ctx") % 2

    def fill(weights):
        for number, ref in enumerate(weights):
            result = jnp.dot(rows, ref[...], preferred_element_type=jnp.float32)
            result = result.reshape(8, SHARE, BLK).astype(out_ref.dtype)
            out_ref[8 * number : 8 * number + 8] = result

    @pl.when(core == 0)
    def _():
        fill((own_ref, other_ref))

    @pl.when(core == 1)
    def _():
        fill((other_ref, own_ref))

    anchor_ref[...] = rows_ref[:, HALF:, :].reshape(2, BLK, HD)


def block_kernel(
    info_ref, query_ref, keyval_ref, own_ref, other_ref, score_hbm, out_ref, score_ref, done
):
    step = pl.program_id(0)
    core = lax.axis_index("ctx") % 2
    scored = (step == 1) & (core == 0)
    block = jnp.where(step == 0, read(info_ref, 9), read(info_ref, 8))
    mine = block // NB == core
    bias = jnp.where(block % NB != 0, 0.0, masked_score)
    copy = pltpu.make_async_copy(score_hbm, score_ref, done)

    @pl.when((step == 0) & (core == 0))
    def _():
        copy.start()


    def anchor(member):
        return jnp.where(mine, own_ref[member], other_ref[member])

    values = jnp.concatenate([anchor(1), keyval_ref[1]], axis=0)
    key = lax.broadcasted_iota(jnp.int32, (BLK, BLK), 1)
    row = lax.broadcasted_iota(jnp.int32, (BLK, BLK), 0)
    live = key <= row

    def finish(head, former, latter):
        raw = jnp.concatenate([former + bias, jnp.where(live, latter, masked_score)], axis=1)
        _, total, weights = row_softmax(raw)
        result = weigh(weights, values) / total
        out_ref[:, head * HD : (head + 1) * HD] = result.astype(jnp.bfloat16)

    @pl.when(scored)
    def _():
        copy.wait()
        for head, raw in each_head(query_ref, anchor(0)):
            finish(head, raw, score_ref[head])

    @pl.when(jnp.logical_not(scored))
    def _():
        keys = jnp.concatenate([anchor(0), keyval_ref[0]], axis=0)
        for head, raw in each_head(query_ref, keys):
            finish(head, raw[:, :BLK], raw[:, BLK:])


def far(array):
    return pltpu.with_memory_space_constraint(array, pltpu.HBM)


def shaped(shape, dtype):
    return jax.ShapeDtypeStruct(shape, dtype)


def on_device(
    ctx_queries, ctx_keyvals, block_map, window_reach, win_queries, win_keyvals, out_weight
):
    other_keyvals = lax.ppermute(ctx_keyvals, "ctx", core_swap)
    halves = win_queries.reshape(2, 4, 2, SHARE, HEADS * HD)
    queries, keyvals, window, info = pl.pallas_call(
        fetch_kernel,
        out_shape=(
            shaped((2, 4, SHARE, HEADS * HD), jnp.bfloat16),
            shaped((2, 2 * BLK, HD), jnp.bfloat16),
            shaped((2, BLK, HD), jnp.bfloat16),
            shaped((16, HD), jnp.float32),
        ),
        in_specs=[hbm] * 5,
        out_specs=(vmem,) * 4,
        scratch_shapes=[
            pltpu.SMEM((2 * NB,), jnp.int32),
            pltpu.SMEM((2,), jnp.int32),
            pltpu.SemaphoreType.DMA((5,)),
        ],
        compiler_params=params(),
        cost_estimate=cost(2**24, 2**15, 2**21),
        name="window_fetch",
    )(
        *(far(array) for array in (block_map, window_reach, halves, ctx_keyvals, win_keyvals))
    )
    queries, other_keyvals, out_weight = lax.optimization_barrier(
        (queries, other_keyvals, out_weight)
    )
    other_weight = lax.ppermute(out_weight, "ctx", core_swap)
    send, own_mean, own_level, scores = pl.pallas_call(
        window_kernel,
        out_shape=(
            shaped((CHIPS, SEND_ROWS, HD), jnp.bfloat16),
            shaped((HALF, HD), jnp.float32),
            shaped((8, HALF), jnp.float32),
            pltpu.HBM((HEADS, BLK, BLK), jnp.float32),
        ),
        in_specs=[vmem] * 5 + [hbm],
        out_specs=(vmem, vmem, vmem, hbm),
        scratch_shapes=[
            pltpu.VMEM((HEADS, BLK, BLK), jnp.float32),
            pltpu.VMEM((BLK, HEADS * HD), jnp.bfloat16),
            pltpu.SemaphoreType.DMA((2,)),
        ],
        compiler_params=params(),
        cost_estimate=cost(2**29, 2**20, 2**21),
        name="window_parts",
    )(info, queries, keyvals, other_keyvals, window, far(ctx_queries))
    send, other_weight = lax.optimization_barrier((send, other_weight))
    got = lax.all_to_all(send, "ctx", 0, 0, axis_index_groups=same_core, tiled=True)
    share = pl.pallas_call(
        combine_kernel,
        out_shape=shaped((CHIPS, SHARE_ROWS, HD), jnp.bfloat16),
        in_specs=[vmem] * 6,
        out_specs=vmem,
        scratch_shapes=[
            pltpu.VMEM((HALF, HD), jnp.float32),
            pltpu.VMEM((8, HALF), jnp.float32),
        ],
        compiler_params=params(),
        cost_estimate=cost(2**20, 2**12, 2**20),
        name="window_join",
    )(info, got, own_mean, own_level, queries, window)
    rows = lax.all_to_all(share, "ctx", 0, 0, axis_index_groups=same_core, tiled=True)
    shares, anchor = pl.pallas_call(
        project_kernel,
        out_shape=(
            shaped((2 * 8, SHARE, BLK), jnp.bfloat16),
            shaped((2, BLK, HD), jnp.bfloat16),
        ),
        in_specs=[vmem, vmem, vmem],
        out_specs=(vmem, vmem),
        compiler_params=params(),
        cost_estimate=cost(2**28, 0, 2**21),
        name="project",
    )(rows, out_weight, other_weight)
    summands = lax.all_to_all(
        shares, ("ctx", "tp"), 0, 0, axis_index_groups=same_chip, tiled=True
    )
    other_anchor = lax.ppermute(anchor, "ctx", core_swap)
    context_attn = pl.pallas_call(
        block_kernel,
        out_shape=shaped((2 * BLK, HEADS * HD), jnp.bfloat16),
        grid=(2,),
        in_specs=[
            vmem,
            pl.BlockSpec((BLK, HEADS * HD), lambda step: (1 - step, 0)),
            pl.BlockSpec((2, BLK, HD), lambda step: (0, 1 - step, 0)),
            pl.BlockSpec((2, BLK, HD), lambda step: (0, 0, 0)),
            pl.BlockSpec((2, BLK, HD), lambda step: (0, 0, 0)),
            hbm,
        ],
        out_specs=pl.BlockSpec((BLK, HEADS * HD), lambda step: (1 - step, 0)),
        scratch_shapes=[
            pltpu.VMEM((HEADS, BLK, BLK), jnp.float32),
            pltpu.SemaphoreType.DMA,
        ],
        compiler_params=params(),
        cost_estimate=cost(2**30, 2**21, 2**22),
        name="block_attention",
    )(info, ctx_queries, ctx_keyvals, anchor, other_anchor, far(scores))
    summands, context_attn = lax.optimization_barrier((summands, context_attn))
    summands = summands.reshape(2, 8, SHARE, BLK).astype(jnp.float32)
    window_proj = jnp.sum(summands, axis=1).reshape(2 * SHARE, BLK)
    return (context_attn, window_proj)


def solution(mesh):
    return jax.shard_map(
        on_device,
        mesh=mesh,
        in_specs=(
            P("ctx", "tp"),
            P(None, "ctx", "tp"),
            P(),
            P(),
            P(None, None, "tp"),
            P(None, None, None, "tp"),
            P("tp", "ctx"),
        ),
        out_specs=(P("ctx", "tp"), P("tp", "ctx")),
        check_vma=False,
    )
```

```python
import math

import jax
import jax.numpy as jnp
from jax import lax
from jax.experimental import pallas as pl
from jax.experimental.pallas import tpu as pltpu
from jax.sharding import PartitionSpec as P

HD = 128
HEADS = 8
BLK = 256
NB = 32
CHIPS = 16
HALF = 128
STAT = 16
PIECE = 32
SHARE = 32
SCALE = 1.0 / math.sqrt(HD)
SCALE2 = SCALE * math.log2(math.e)
AHEAD = 1
masked_score = -1e30

SEND_ROWS = HALF + STAT + PIECE
SHARE_ROWS = HALF + PIECE

same_core = [
    [(place + core * CHIPS // 2) % CHIPS * 2 + core for place in range(CHIPS)]
    for core in range(2)
]
same_chip = [
    [(chip * 2 + core) * 8 + plane for core in range(2) for plane in range(8)]
    for chip in range(CHIPS)
]
core_swap = [(device, device ^ 1) for device in range(2 * CHIPS)]

vmem = pl.BlockSpec(memory_space=pltpu.VMEM)
hbm = pl.BlockSpec(memory_space=pltpu.HBM)


def params(room=40):
    return pltpu.CompilerParams(vmem_limit_bytes=room * 2**20)


def cost(flops, exps, size):
    return pl.CostEstimate(flops=flops, transcendentals=exps, bytes_accessed=size)


def split_three(value):
    high = value.astype(jnp.bfloat16)
    rest = value - high.astype(jnp.float32)
    middle = rest.astype(jnp.bfloat16)
    low = (rest - middle.astype(jnp.float32)).astype(jnp.bfloat16)
    return high, middle, low


def dot_nt(left, right):
    return lax.dot_general(
        left, right, (((1,), (1,)), ((), ())), preferred_element_type=jnp.float32
    )


def row_softmax(raw):
    top = jnp.max(raw, axis=1, keepdims=True)
    weights = jnp.exp2((raw - top) * SCALE2)
    return top, jnp.sum(weights, axis=1, keepdims=True), weights


def weigh(weights, values):
    return jnp.dot(weights.astype(jnp.bfloat16), values, preferred_element_type=jnp.float32)


def each_head(query_ref, keys):
    ready = []
    for head in range(HEADS + AHEAD):
        if head < HEADS:
            ready.append(dot_nt(query_ref[:, head * HD : (head + 1) * HD], keys))
        if head >= AHEAD:
            yield head - AHEAD, ready.pop(0)


def read(info_ref, number):
    return jnp.max(info_ref[number : number + 1, :]).astype(jnp.int32)


def own_window(query_ref, window_ref):
    position = lax.axis_index("ctx")
    core = position % 2
    chip = (position // 2 + core * (CHIPS // 2)) % CHIPS
    lanes = pl.ds(pl.multiple_of(chip // 2 * HD, HD), HD)
    query = query_ref[chip % 2, :, :, lanes].reshape(HALF, HD)
    raw = dot_nt(query, window_ref[0])
    key = lax.broadcasted_iota(jnp.int32, raw.shape, 1)
    row = lax.broadcasted_iota(jnp.int32, raw.shape, 0)
    row = row // SHARE * (2 * SHARE) + core * SHARE + row % SHARE
    raw = jnp.where(key <= row, raw, masked_score)
    top, total, weights = row_softmax(raw)
    mean = weigh(weights, window_ref[1]) / total
    level = jnp.broadcast_to(top * SCALE + jnp.log(total), (HALF, HALF)).T
    return mean, level[:8]


def fetch_kernel(
    map_hbm,
    reach_hbm,
    query_hbm,
    keyval_hbm,
    window_hbm,
    query_ref,
    keyval_ref,
    window_ref,
    info_ref,
    map_ref,
    reach_ref,
    done,
):
    position = lax.axis_index("ctx")
    core = position % 2
    chip = (position // 2 + core * (CHIPS // 2)) % CHIPS
    copies = [
        pltpu.make_async_copy(source, target, done.at[number])
        for number, (source, target) in enumerate(
            (
                (map_hbm, map_ref),
                (reach_hbm, reach_ref),
                (query_hbm.at[:, :, core], query_ref),
                (keyval_hbm, keyval_ref),
                (window_hbm.at[chip % 2], window_ref),
            )
        )
    ]
    for copy in copies:
        copy.start()
    for copy in copies[:2]:
        copy.wait()
    partner = position + 1 - 2 * core

    def put(number, value):
        info_ref[number : number + 1, :] = jnp.full((1, HD), value.astype(jnp.float32))

    holder = jnp.int32(0)
    for number in range(2 * NB):
        holder = jnp.where(map_ref[number] == core * NB, number // 4, holder)
    put(0, (holder + core * (CHIPS // 2)) % CHIPS)
    for part, device in enumerate((position, partner)):
        put(1 + part, map_ref[2 * device] // NB)
        for context in range(2):
            slot = jnp.where(map_ref[2 * device] // NB == context, 0, 1)
            place = map_ref[2 * device + slot] - NB * context
            put(3 + 2 * context + part, jnp.where(place < reach_ref[context], 1, 0))
    slot = jnp.where(map_ref[2 * position] // NB == core, 0, 1)
    put(7, map_ref[2 * position + slot] - NB * core)
    put(8, map_ref[2 * position])
    put(9, map_ref[2 * position + 1])
    for copy in copies[2:]:
        copy.wait()


def window_kernel(
    info_ref,
    query_ref,
    own_ref,
    other_ref,
    window_ref,
    rows_hbm,
    send_ref,
    mean_ref,
    level_ref,
    score_hbm,
    score_ref,
    rows_ref,
    done,
):
    core = lax.axis_index("ctx") % 2
    copy = pltpu.make_async_copy(rows_hbm.at[:BLK], rows_ref, done.at[0])

    @pl.when(core == 0)
    def _():
        copy.start()

    slots = [read(info_ref, 1 + part) for part in range(2)]

    def block_rows(part, context):
        slot = slots[part] if context == 0 else 1 - slots[part]
        return pl.ds(pl.multiple_of(slot * BLK, BLK), BLK)

    sources = (own_ref, other_ref)
    lane = lax.broadcasted_iota(jnp.int32, (BLK, HD), 1)
    columns = jnp.zeros((BLK, HD), jnp.float32)
    steps = [(context, pair) for context in range(2) for pair in range(HEADS // 2)]
    keys = []
    values = []
    biases = []
    for context in range(2):
        rows = [block_rows(part, context) for part in range(2)]
        keys.append(
            jnp.concatenate([ref[0, taken, :] for ref, taken in zip(sources, rows)], axis=0)
        )
        values.append([ref[1, taken, :] for ref, taken in zip(sources, rows)])
        biases.append(
            [
                jnp.where(read(info_ref, number) == 1, 0.0, masked_score)
                for number in (3 + 2 * context, 4 + 2 * context)
            ]
        )

    def score(step):
        context, pair = steps[step]
        query = jnp.concatenate(
            [
                query_ref[context, :, :, head * HD : (head + 1) * HD].reshape(HALF, HD)
                for head in (2 * pair, 2 * pair + 1)
            ],
            axis=0,
        )
        return dot_nt(query, keys[context])

    first = read(info_ref, 7) == 0
    own_rows, other_rows = [
        pl.ds(pl.multiple_of((slots[part] ^ core) * BLK, BLK), BLK) for part in range(2)
    ]
    for member in range(2):
        block = jnp.where(first, own_ref[member, own_rows, :], other_ref[member, other_rows, :])
        send_ref[8 * member : 8 * member + 8, HALF + STAT :, :] = block.reshape(8, PIECE, HD)

    def write_stats(columns, context):
        table = columns.T
        level = table[:HEADS] * SCALE + jnp.log(table[HEADS : 2 * HEADS])
        pieces = [piece.astype(jnp.float32) for piece in split_three(level)]
        row = lax.broadcasted_iota(jnp.int32, (STAT, BLK), 0)
        for pair in range(HEADS // 2):
            stats = jnp.zeros((STAT, BLK), jnp.float32)
            for number, piece in enumerate(pieces):
                stats = jnp.where(row == number, piece[pair : pair + 1], stats)
            stats = stats.astype(jnp.bfloat16)
            for half in range(2):
                target = 2 * (2 * pair + half) + context
                lanes = slice(half * HALF, (half + 1) * HALF)
                send_ref[target, HALF : HALF + STAT, :] = stats[:, lanes]

    ready = [score(step) for step in range(AHEAD)]
    for step, (context, pair) in enumerate(steps):
        if step + AHEAD < len(steps):
            ready.append(score(step + AHEAD))
        raw = ready.pop(0)
        parts = []
        for part in range(2):
            top, total, weights = row_softmax(raw[:, part * BLK : (part + 1) * BLK])
            parts.append(
                (top + biases[context][part], total, weigh(weights, values[context][part]))
            )
        joined = jnp.maximum(parts[0][0], parts[1][0])
        lifts = [jnp.exp2((part[0] - joined) * SCALE2) for part in parts]
        total = parts[0][1] * lifts[0] + parts[1][1] * lifts[1]
        inverse = 1.0 / total
        mean = parts[0][2] * (lifts[0] * inverse) + parts[1][2] * (lifts[1] * inverse)
        mean = mean.astype(jnp.bfloat16)
        for half in range(2):
            target = 2 * (2 * pair + half) + context
            send_ref[target, :HALF, :] = mean[half * HALF : (half + 1) * HALF]
        columns = jnp.where(lane == pair, joined, columns)
        columns = jnp.where(lane == HEADS + pair, total, columns)
        if pair == HEADS // 2 - 1:
            write_stats(columns, context)

    @pl.when(core == 0)
    def _():
        mean_ref[...], level_ref[...] = own_window(query_ref, window_ref)
        copy.wait()
        for head in range(HEADS):
            query = rows_ref[:, head * HD : (head + 1) * HD]
            score_ref[head] = dot_nt(query, own_ref[0, :BLK, :])
        copy_out = pltpu.make_async_copy(score_ref, score_hbm, done.at[1])
        copy_out.start()
        copy_out.wait()


def combine_kernel(
    info_ref, got_ref, mean_in, level_in, query_ref, window_ref, share_ref, mean_ref, level_ref
):
    core = lax.axis_index("ctx") % 2

    @pl.when(core == 0)
    def _():
        mean_ref[...] = mean_in[...]
        level_ref[...] = level_in[...]

    @pl.when(core == 1)
    def _():
        mean_ref[...], level_ref[...] = own_window(query_ref, window_ref)

    levels = []
    for source in range(CHIPS):
        stats = got_ref[source, HALF : HALF + STAT, :].astype(jnp.float32)
        levels.append(stats[0:1] + stats[1:2] + stats[2:3])
    levels.append(level_ref[0:1, :])
    levels = jnp.concatenate(levels, axis=0)
    lifts = jnp.exp(levels - jnp.max(levels, axis=0, keepdims=True))
    lifts = lifts / jnp.sum(lifts, axis=0, keepdims=True)
    count = 3 * (CHIPS + 1)
    source_of = lax.broadcasted_iota(jnp.int32, (count, (CHIPS + 1) * HALF), 0) % (CHIPS + 1)
    column = lax.broadcasted_iota(jnp.int32, (count, (CHIPS + 1) * HALF), 1) // HALF
    spread = jnp.where(source_of == column, 1.0, 0.0).astype(jnp.bfloat16)
    wide = lax.dot_general(
        jnp.concatenate(split_three(lifts), axis=0),
        spread,
        (((0,), (0,)), ((), ())),
        preferred_element_type=jnp.float32,
    )
    joined = mean_ref[...] * wide[:, CHIPS * HALF :]
    for source in range(CHIPS):
        part = got_ref[source, :HALF, :].astype(jnp.float32)
        joined = joined + part * wide[:, source * HALF : (source + 1) * HALF]
    result = joined.astype(jnp.bfloat16)
    piece = got_ref[read(info_ref, 0), HALF + STAT :, :]
    for target in range(CHIPS):
        share_ref[target, :HALF, :] = result
        share_ref[target, HALF:, :] = piece


def project_kernel(rows_ref, own_ref, other_ref, out_ref, anchor_ref):
    rows = jnp.concatenate(
        [
            jnp.concatenate(
                [rows_ref[2 * head + context, :HALF, :] for head in range(HEADS)], axis=1
            )
            for context in range(2)
        ],
        axis=0,
    )
    core = lax.axis_index("ctx") % 2

    def fill(weights):
        for number, ref in enumerate(weights):
            result = jnp.dot(rows, ref[...], preferred_element_type=jnp.float32)
            result = result.reshape(8, SHARE, BLK).astype(out_ref.dtype)
            out_ref[8 * number : 8 * number + 8] = result

    @pl.when(core == 0)
    def _():
        fill((own_ref, other_ref))

    @pl.when(core == 1)
    def _():
        fill((other_ref, own_ref))

    anchor_ref[...] = rows_ref[:, HALF:, :].reshape(2, BLK, HD)


def block_kernel(
    info_ref, query_ref, keyval_ref, own_ref, other_ref, score_hbm, out_ref, score_ref, done
):
    step = pl.program_id(0)
    core = lax.axis_index("ctx") % 2
    scored = (step == 1) & (core == 0)
    block = jnp.where(step == 0, read(info_ref, 9), read(info_ref, 8))
    mine = block // NB == core
    bias = jnp.where(block % NB != 0, 0.0, masked_score)
    copy = pltpu.make_async_copy(score_hbm, score_ref, done)

    @pl.when((step == 0) & (core == 0))
    def _():
        copy.start()


    def anchor(member):
        return jnp.where(mine, own_ref[member], other_ref[member])

    values = jnp.concatenate([anchor(1), keyval_ref[1]], axis=0)
    key = lax.broadcasted_iota(jnp.int32, (BLK, BLK), 1)
    row = lax.broadcasted_iota(jnp.int32, (BLK, BLK), 0)
    live = key <= row

    def finish(head, former, latter):
        raw = jnp.concatenate([former + bias, jnp.where(live, latter, masked_score)], axis=1)
        _, total, weights = row_softmax(raw)
        result = weigh(weights, values) / total
        out_ref[:, head * HD : (head + 1) * HD] = result.astype(jnp.bfloat16)

    @pl.when(scored)
    def _():
        copy.wait()
        for head, raw in each_head(query_ref, anchor(0)):
            finish(head, raw, score_ref[head])

    @pl.when(jnp.logical_not(scored))
    def _():
        keys = jnp.concatenate([anchor(0), keyval_ref[0]], axis=0)
        for head, raw in each_head(query_ref, keys):
            finish(head, raw[:, :BLK], raw[:, BLK:])


def far(array):
    return pltpu.with_memory_space_constraint(array, pltpu.HBM)


def shaped(shape, dtype):
    return jax.ShapeDtypeStruct(shape, dtype)


def on_device(
    ctx_queries, ctx_keyvals, block_map, window_reach, win_queries, win_keyvals, out_weight
):
    other_keyvals = lax.ppermute(ctx_keyvals, "ctx", core_swap)
    halves = win_queries.reshape(2, 4, 2, SHARE, HEADS * HD)
    queries, keyvals, window, info = pl.pallas_call(
        fetch_kernel,
        out_shape=(
            shaped((2, 4, SHARE, HEADS * HD), jnp.bfloat16),
            shaped((2, 2 * BLK, HD), jnp.bfloat16),
            shaped((2, BLK, HD), jnp.bfloat16),
            shaped((16, HD), jnp.float32),
        ),
        in_specs=[hbm] * 5,
        out_specs=(vmem,) * 4,
        scratch_shapes=[
            pltpu.SMEM((2 * NB,), jnp.int32),
            pltpu.SMEM((2,), jnp.int32),
            pltpu.SemaphoreType.DMA((5,)),
        ],
        compiler_params=params(),
        cost_estimate=cost(2**24, 2**15, 2**21),
        name="window_fetch",
    )(
        *(far(array) for array in (block_map, window_reach, halves, ctx_keyvals, win_keyvals))
    )
    queries, other_keyvals, out_weight = lax.optimization_barrier(
        (queries, other_keyvals, out_weight)
    )
    other_weight = lax.ppermute(out_weight, "ctx", core_swap)
    send, own_mean, own_level, scores = pl.pallas_call(
        window_kernel,
        out_shape=(
            shaped((CHIPS, SEND_ROWS, HD), jnp.bfloat16),
            shaped((HALF, HD), jnp.float32),
            shaped((8, HALF), jnp.float32),
            pltpu.HBM((HEADS, BLK, BLK), jnp.float32),
        ),
        in_specs=[vmem] * 5 + [hbm],
        out_specs=(vmem, vmem, vmem, hbm),
        scratch_shapes=[
            pltpu.VMEM((HEADS, BLK, BLK), jnp.float32),
            pltpu.VMEM((BLK, HEADS * HD), jnp.bfloat16),
            pltpu.SemaphoreType.DMA((2,)),
        ],
        compiler_params=params(),
        cost_estimate=cost(2**29, 2**20, 2**21),
        name="window_parts",
    )(info, queries, keyvals, other_keyvals, window, far(ctx_queries))
    send, other_weight = lax.optimization_barrier((send, other_weight))
    got = lax.all_to_all(send, "ctx", 0, 0, axis_index_groups=same_core, tiled=True)
    share = pl.pallas_call(
        combine_kernel,
        out_shape=shaped((CHIPS, SHARE_ROWS, HD), jnp.bfloat16),
        in_specs=[vmem] * 6,
        out_specs=vmem,
        scratch_shapes=[
            pltpu.VMEM((HALF, HD), jnp.float32),
            pltpu.VMEM((8, HALF), jnp.float32),
        ],
        compiler_params=params(),
        cost_estimate=cost(2**20, 2**12, 2**20),
        name="window_join",
    )(info, got, own_mean, own_level, queries, window)
    rows = lax.all_to_all(share, "ctx", 0, 0, axis_index_groups=same_core, tiled=True)
    shares, anchor = pl.pallas_call(
        project_kernel,
        out_shape=(
            shaped((2 * 8, SHARE, BLK), jnp.bfloat16),
            shaped((2, BLK, HD), jnp.bfloat16),
        ),
        in_specs=[vmem, vmem, vmem],
        out_specs=(vmem, vmem),
        compiler_params=params(),
        cost_estimate=cost(2**28, 0, 2**21),
        name="project",
    )(rows, out_weight, other_weight)
    summands = lax.all_to_all(
        shares, ("ctx", "tp"), 0, 0, axis_index_groups=same_chip, tiled=True
    )
    other_anchor = lax.ppermute(anchor, "ctx", core_swap)
    context_attn = pl.pallas_call(
        block_kernel,
        out_shape=shaped((2 * BLK, HEADS * HD), jnp.bfloat16),
        grid=(2,),
        in_specs=[
            vmem,
            pl.BlockSpec((BLK, HEADS * HD), lambda step: (1 - step, 0)),
            pl.BlockSpec((2, BLK, HD), lambda step: (0, 1 - step, 0)),
            pl.BlockSpec((2, BLK, HD), lambda step: (0, 0, 0)),
            pl.BlockSpec((2, BLK, HD), lambda step: (0, 0, 0)),
            hbm,
        ],
        out_specs=pl.BlockSpec((BLK, HEADS * HD), lambda step: (1 - step, 0)),
        scratch_shapes=[
            pltpu.VMEM((HEADS, BLK, BLK), jnp.float32),
            pltpu.SemaphoreType.DMA,
        ],
        compiler_params=params(),
        cost_estimate=cost(2**30, 2**21, 2**22),
        name="block_attention",
    )(info, ctx_queries, ctx_keyvals, anchor, other_anchor, far(scores))
    summands, context_attn = lax.optimization_barrier((summands, context_attn))
    summands = summands.reshape(2, 8, SHARE, BLK).astype(jnp.float32)
    window_proj = jnp.sum(summands, axis=1).reshape(2 * SHARE, BLK)
    return (context_attn, window_proj)


def solution(mesh):
    return jax.shard_map(
        on_device,
        mesh=mesh,
        in_specs=(
            P("ctx", "tp"),
            P(None, "ctx", "tp"),
            P(),
            P(),
            P(None, None, "tp"),
            P(None, None, None, "tp"),
            P("tp", "ctx"),
        ),
        out_specs=(P("ctx", "tp"), P("tp", "ctx")),
        check_vma=False,
    )
```
